256 devices in a mesh: dp: 8 (over y_lo, x), space: 32 (over y_hi, z, core).
Axes of the slice: x: 4, y: 4 (y_hi: 2, y_lo: 2; y = y_hi * 2 + y_lo), z: 8, core: 2. Of those that a mesh axis runs over, the one named last changes fastest.
Arguments:
- cells: bfloat16 [8, 32768, 256], P('dp', 'space'), may hold values from -6 to 6
- cotangent: bfloat16 [8, 32768, 256], P('dp', 'space'), may hold values from -6 to 6
- cell_count: int32 [8, 32], P('dp', 'space'), may hold values from 1 to 1024, 24576 in all within a row
- first_norm_gain: float32 [256], replicated, may hold values from 0.5 to 1.5
- first_norm_bias: float32 [256], replicated, may hold values from -1.2 to 1.2
- w_fx: bfloat16 [256, 256], replicated, may hold values from -0.375 to 0.375
- w_x: bfloat16 [256, 256], replicated, may hold values from -0.375 to 0.375
- w_slice: bfloat16 [32, 64], replicated, may hold values from -1 to 1
- temper: float32 [8], replicated, may hold values from 0.25 to 1
- query_weight: float32 [32, 32], replicated, may hold values from -1 to 1
- key_weight: float32 [32, 32], replicated, may hold values from -1 to 1
- value_weight: float32 [32, 32], replicated, may hold values from -1 to 1
- w_out: bfloat16 [256, 256], replicated, may hold values from -0.375 to 0.375
- second_norm_gain: float32 [256], replicated, may hold values from 0.5 to 1.5
- second_norm_bias: float32 [256], replicated, may hold values from -1.2 to 1.2
- w_up: bfloat16 [256, 256], replicated, may hold values from -0.375 to 0.375
- w_down: bfloat16 [256, 256], replicated, may hold values from -0.375 to 0.375
Outputs:
- layer_out: bfloat16 [8, 32768, 256], P('dp', 'space')
- grad_cells: bfloat16 [8, 32768, 256], P('dp', 'space')
- grad_ln1_gain: float32 [256], replicated
- grad_ln1_bias: float32 [256], replicated
- grad_fx: float32 [256, 256], replicated
- grad_x: float32 [256, 256], replicated
- grad_slice: float32 [32, 64], replicated
- grad_temper: float32 [8], replicated
- grad_q: float32 [32, 32], replicated
- grad_k: float32 [32, 32], replicated
- grad_v: float32 [32, 32], replicated
- grad_out: float32 [256, 256], replicated
- grad_ln2_gain: float32 [256], replicated
- grad_ln2_bias: float32 [256], replicated
- grad_up: float32 [256, 256], replicated
- grad_down: float32 [256, 256], replicated
The draws below stay inside these ranges and needn't reach their ends.
Inputs may be any that keep to these rules, and one draw needn't show every extreme that they name: The first cell_count[s, j] of shard j's 1024 slots are live cells, the rest are padding; every scenario has a full shard.
All inputs are finite; a program needn't handle non-finite values.
Results may differ from the reference program's by a relative error of at most 0.034.
The reference program's roundings to bfloat16 on the way count: a program that leaves them out, or rounds other values in their place, can miss the bound.
Values sent between devices are 32-bit elements; how exact they have to be, the bound alone decides.
No kernel may reach another device: no remote copies, remote signals or barrier semaphores. Data moves between devices by JAX's collectives and lax.ppermute only.
A program may use at most 64 MiB of HBM per device.

```python
import math
import jax
import jax.numpy as jnp
import numpy as np
from jax import lax

CELL_WIDTH = 256
ATTENTION_HEADS = 8
SLICES = 64
HEAD_SIZE = 32
CELL_DEV = 1024
SHARDS = 32
SCEN = 8
CELLS = 32768


def level_of(rng, extent, shards, least, largest):
    gain, own = 1.0, jax.random.fold_in(rng, 6)
    for position, shards_of in shards:
        heights = jnp.exp(jax.random.uniform(jax.random.fold_in(own, position), (shards_of,), jnp.float32, least / len(shards), largest / len(shards)))
        gain = gain * jnp.repeat(heights, extent[position] // shards_of).reshape([-1 if axis == position else 1 for axis in range(len(extent))])
    return gain


def length_profile(number_of, total, bound, lean):
    weights = [(1 << 20) // math.isqrt(standing ** lean) + 1 for standing in range(2, number_of + 1)]
    rest, given = total - bound - (number_of - 1), [1] * (number_of - 1)
    while rest > 0:
        movable = [i for i in range(number_of - 1) if given[i] < bound]
        whole, budget = sum([weights[i] for i in movable]), rest
        for i in movable:
            extra = min(bound - given[i], max(1, budget * weights[i] // whole), rest)
            given[i] = given[i] + extra
            rest = rest - extra
    return np.array([bound] + given)


def ragged_sizes(stream_key, number_of, total, reach, lean):
    if number_of == 2:
        one = jax.random.randint(stream_key, (), max(1, total - reach), min(reach, total - 1) + 1)
        return jnp.stack([one, total - one])
    lengths = jnp.asarray(length_profile(number_of, total, reach, lean), jnp.int32)
    twos = (number_of - 1) // 2
    giver, taker = lengths[1:1 + 2 * twos:2], lengths[2:2 + 2 * twos:2]
    margin = jnp.minimum(giver - 1, reach - taker)
    shifted = jax.random.randint(jax.random.fold_in(stream_key, 1), (twos,), 0, 1 << 20) % (margin + 1)
    lengths = lengths.at[1:1 + 2 * twos:2].set(giver - shifted).at[2:2 + 2 * twos:2].set(taker + shifted)
    return lengths[jax.random.permutation(jax.random.fold_in(stream_key, 2), number_of)]


def centred(stream_key, extent, width, bound, cuts=(), kind=jnp.bfloat16):
    factor_of = level_of(stream_key, extent, cuts, -0.22, 0.18) if cuts else 1.0
    entries = jax.random.normal(stream_key, extent, jnp.float32) * width * factor_of
    return jnp.minimum(jnp.maximum(entries, -bound), bound).astype(kind)


def setup_inputs(seed: int = 0) -> dict:
    keys = jax.random.split(jax.random.key(seed), 18)
    cells = centred(keys[0], (SCEN, CELLS, CELL_WIDTH), 1.0, 6.0, ((0, 8), (1, 32)))
    cotangent = centred(keys[1], (SCEN, CELLS, CELL_WIDTH), 1.0, 6.0, ((0, 8), (1, 32)))
    cell_count = jax.vmap(lambda own: ragged_sizes(own, SHARDS, SHARDS * CELL_DEV * 3 // 4, CELL_DEV, 1))(jax.random.split(keys[2], SCEN)).reshape((SCEN, SHARDS)).astype(jnp.int32)
    first_norm_gain = jnp.clip(1.0 + 0.1 * jax.random.normal(keys[3], (CELL_WIDTH,), jnp.float32), 0.5, 1.5)
    first_norm_bias = centred(keys[4], (CELL_WIDTH,), 0.3, 1.2, (), jnp.float32)
    w_fx = centred(keys[5], (CELL_WIDTH, CELL_WIDTH), CELL_WIDTH ** -0.5, 0.375)
    w_x = centred(keys[6], (CELL_WIDTH, CELL_WIDTH), CELL_WIDTH ** -0.5, 0.375)
    w_slice = centred(keys[7], (HEAD_SIZE, SLICES), HEAD_SIZE ** -0.5, 1.0)
    temper = jnp.clip(jnp.exp(jax.random.uniform(keys[8], (ATTENTION_HEADS,), jnp.float32, math.log(0.25), math.log(1.0))), 0.25, 1.0)
    query_weight = centred(keys[9], (HEAD_SIZE, HEAD_SIZE), HEAD_SIZE ** -0.5, 1.0, (), jnp.float32)
    key_weight = centred(keys[10], (HEAD_SIZE, HEAD_SIZE), HEAD_SIZE ** -0.5, 1.0, (), jnp.float32)
    value_weight = centred(keys[11], (HEAD_SIZE, HEAD_SIZE), HEAD_SIZE ** -0.5, 1.0, (), jnp.float32)
    w_out = centred(keys[12], (CELL_WIDTH, CELL_WIDTH), CELL_WIDTH ** -0.5, 0.375)
    second_norm_gain = jnp.clip(1.0 + 0.1 * jax.random.normal(keys[13], (CELL_WIDTH,), jnp.float32), 0.5, 1.5)
    second_norm_bias = centred(keys[14], (CELL_WIDTH,), 0.3, 1.2, (), jnp.float32)
    w_up = centred(keys[15], (CELL_WIDTH, CELL_WIDTH), CELL_WIDTH ** -0.5, 0.375)
    w_down = centred(keys[16], (CELL_WIDTH, CELL_WIDTH), CELL_WIDTH ** -0.5, 0.375)
    return {"cells": cells, "cotangent": cotangent, "cell_count": cell_count, "first_norm_gain": first_norm_gain, "first_norm_bias": first_norm_bias, "w_fx": w_fx, "w_x": w_x, "w_slice": w_slice, "temper": temper, "query_weight": query_weight, "key_weight": key_weight, "value_weight": value_weight, "w_out": w_out, "second_norm_gain": second_norm_gain, "second_norm_bias": second_norm_bias, "w_up": w_up, "w_down": w_down}


EPS = 1e-05

def expanded_rows(value):
    return lax.optimization_barrier(value.astype(jnp.bfloat16)).astype(jnp.float32)

def norm_forward_pass(input_rows, norm_gain, norm_shift):
    input_rows = input_rows.astype(jnp.float32)
    centered_input = input_rows - lax.optimization_barrier(jnp.mean(input_rows, axis=-1, keepdims=True))
    inverse_deviation = lax.rsqrt(lax.optimization_barrier(jnp.mean(centered_input * centered_input, axis=-1, keepdims=True)) + EPS)
    normalized_input = centered_input * inverse_deviation
    return (normalized_input, inverse_deviation, (normalized_input * norm_gain + norm_shift).astype(jnp.bfloat16))

def norm_backward_pass(norm_input_gradient, normalized_input, inverse_deviation, norm_gain):
    normalized_gradient = norm_input_gradient * norm_gain
    return inverse_deviation * (normalized_gradient - lax.optimization_barrier(jnp.mean(normalized_gradient, axis=-1, keepdims=True)) - normalized_input * lax.optimization_barrier(jnp.mean(normalized_gradient * normalized_input, axis=-1, keepdims=True)))

def front(input_rows, count, first_norm_gain, first_norm_bias, w_fx, w_x, w_slice, temper):
    token_count = input_rows.shape[0]
    first_normalized_input, first_inverse_deviation, first_normed_rows = norm_forward_pass(input_rows, first_norm_gain, first_norm_bias)
    cell_features = jnp.dot(first_normed_rows, w_fx, preferred_element_type=jnp.float32).astype(jnp.bfloat16)
    hidden_activations = jnp.dot(first_normed_rows, w_x, preferred_element_type=jnp.float32).astype(jnp.bfloat16)
    slice_logits = jnp.dot(hidden_activations.reshape(token_count * ATTENTION_HEADS, HEAD_SIZE), w_slice, preferred_element_type=jnp.float32)
    slice_logits = slice_logits.reshape(token_count, ATTENTION_HEADS, SLICES) / temper[None, :, None]
    live = (jnp.arange(token_count, dtype=jnp.int32) < count).astype(jnp.float32)
    attention_probabilities = jax.nn.softmax(slice_logits, axis=-1) * live[:, None, None]
    return (first_normalized_input, first_inverse_deviation, first_normed_rows, cell_features, hidden_activations, slice_logits, attention_probabilities)

def pool(attention_probabilities, cell_features):
    token_count = attention_probabilities.shape[0]
    slice_numerator = jnp.einsum('fup,fuk->upk', expanded_rows(attention_probabilities), cell_features.reshape(token_count, ATTENTION_HEADS, HEAD_SIZE).astype(jnp.float32))
    return (slice_numerator, lax.optimization_barrier(jnp.sum(attention_probabilities, axis=0)))

def mix_tokens(slice_tokens, query_weight, key_weight, value_weight):
    maximum_logit = lax.Precision.HIGHEST
    query_rows = jnp.einsum('zcr,rt->zct', slice_tokens, query_weight, precision=maximum_logit)
    key_rows = jnp.einsum('zcr,rt->zct', slice_tokens, key_weight, precision=maximum_logit)
    value_rows = jnp.einsum('zcr,rt->zct', slice_tokens, value_weight, precision=maximum_logit)
    attention_scores = jnp.einsum('pfq,plq->pfl', query_rows, key_rows, precision=maximum_logit) * HEAD_SIZE ** (-0.5)
    return jnp.einsum('paz,pzy->pay', jax.nn.softmax(attention_scores, axis=-1), value_rows, precision=maximum_logit)

def middle(input_rows, attention_probabilities, mixed_token_batch, incoming_gradients, w_out, second_norm_gain, second_norm_bias, w_up, w_down):
    token_count = input_rows.shape[0]
    slice_weights = expanded_rows(attention_probabilities)
    spread_tokens = jnp.einsum('wqj,qja->wqa', slice_weights, mixed_token_batch.astype(jnp.float32)).reshape(token_count, CELL_WIDTH).astype(jnp.bfloat16)
    residual_rows = (input_rows.astype(jnp.float32) + jnp.dot(spread_tokens, w_out, preferred_element_type=jnp.float32)).astype(jnp.bfloat16)
    second_normalized_input, second_inverse_deviation, second_normed_rows = norm_forward_pass(residual_rows, second_norm_gain, second_norm_bias)
    up = jnp.dot(second_normed_rows, w_up, preferred_element_type=jnp.float32)
    act, gelu_back = jax.vjp(jax.nn.gelu, up)
    act_b = act.astype(jnp.bfloat16)
    layer = (residual_rows.astype(jnp.float32) + jnp.dot(act_b, w_down, preferred_element_type=jnp.float32)).astype(jnp.bfloat16)
    grad_down = jnp.dot(act_b.T, incoming_gradients, preferred_element_type=jnp.float32)
    g_act = jnp.dot(incoming_gradients, w_down.T, preferred_element_type=jnp.float32)
    g_up = gelu_back(g_act)[0].astype(jnp.bfloat16)
    grad_up = jnp.dot(second_normed_rows.T, g_up, preferred_element_type=jnp.float32)
    second_norm_gradient = jnp.dot(g_up, w_up.T, preferred_element_type=jnp.float32)
    second_gain_gradient = lax.optimization_barrier(jnp.sum(second_norm_gradient * second_normalized_input, axis=0))
    grad_bias2 = lax.optimization_barrier(jnp.sum(second_norm_gradient, axis=0))
    residual_gradient = incoming_gradients.astype(jnp.float32) + norm_backward_pass(second_norm_gradient, second_normalized_input, second_inverse_deviation, second_norm_gain)
    g_resid_b = residual_gradient.astype(jnp.bfloat16)
    grad_out = jnp.dot(spread_tokens.T, g_resid_b, preferred_element_type=jnp.float32)
    spread_gradient = jnp.dot(g_resid_b, w_out.T, preferred_element_type=jnp.float32).astype(jnp.bfloat16)
    token_partial = jnp.einsum('fup,fuk->upk', slice_weights, spread_gradient.reshape(token_count, ATTENTION_HEADS, HEAD_SIZE).astype(jnp.float32))
    return (layer, residual_gradient, spread_gradient, token_partial, (grad_out, second_gain_gradient, grad_bias2, grad_up, grad_down))

def rear(next_value, residual_gradient, spread_gradient, mixed_token_batch, numerator_gradient, g_denom, w_fx, w_x, w_slice, temper, first_norm_gain):
    first_normalized_input, first_inverse_deviation, first_normed_rows, cell_features, hidden_activations, slice_logits, attention_probabilities = next_value
    token_count = attention_probabilities.shape[0]
    slice_weights = expanded_rows(attention_probabilities)
    slice_weight_gradient = jnp.einsum('zbe,ble->zbl', spread_gradient.reshape(token_count, ATTENTION_HEADS, HEAD_SIZE).astype(jnp.float32), mixed_token_batch.astype(jnp.float32))
    slice_weight_gradient = slice_weight_gradient + jnp.einsum('zbe,ble->zbl', cell_features.reshape(token_count, ATTENTION_HEADS, HEAD_SIZE).astype(jnp.float32), numerator_gradient.astype(jnp.float32))
    slice_weight_gradient = slice_weight_gradient + g_denom[None]
    g_logits = attention_probabilities * (slice_weight_gradient - lax.optimization_barrier(jnp.sum(slice_weight_gradient * attention_probabilities, axis=-1, keepdims=True)))
    grad_temper = -lax.optimization_barrier(jnp.sum(g_logits * slice_logits, axis=(0, 2))) / temper
    g_scaled = (g_logits / temper[None, :, None]).astype(jnp.bfloat16).reshape(token_count * ATTENTION_HEADS, SLICES)
    g_mids = jnp.dot(g_scaled, w_slice.T, preferred_element_type=jnp.float32).reshape(token_count, CELL_WIDTH).astype(jnp.bfloat16)
    grad_slice = jnp.dot(hidden_activations.reshape(token_count * ATTENTION_HEADS, HEAD_SIZE).T, g_scaled, preferred_element_type=jnp.float32)
    features_gradient = jnp.einsum('wqj,qja->wqa', slice_weights, numerator_gradient.astype(jnp.float32)).reshape(token_count, CELL_WIDTH).astype(jnp.bfloat16)
    grad_fx = jnp.dot(first_normed_rows.T, features_gradient, preferred_element_type=jnp.float32)
    grad_x = jnp.dot(first_normed_rows.T, g_mids, preferred_element_type=jnp.float32)
    first_norm_gradient = jnp.dot(features_gradient, w_fx.T, preferred_element_type=jnp.float32) + jnp.dot(g_mids, w_x.T, preferred_element_type=jnp.float32)
    first_gain_gradient = lax.optimization_barrier(jnp.sum(first_norm_gradient * first_normalized_input, axis=0))
    grad_bias1 = lax.optimization_barrier(jnp.sum(first_norm_gradient, axis=0))
    row_gradient = (residual_gradient + norm_backward_pass(first_norm_gradient, first_normalized_input, first_inverse_deviation, first_norm_gain)).astype(jnp.bfloat16)
    return (row_gradient, (first_gain_gradient, grad_bias1, grad_fx, grad_x, grad_slice, grad_temper))

def reference(cells, cotangent, cell_count, first_norm_gain, first_norm_bias, w_fx, w_x, w_slice, temper, query_weight, key_weight, value_weight, w_out, second_norm_gain, second_norm_bias, w_up, w_down):
    blocks = SCEN * SHARDS
    rows_all = cells.reshape(blocks, CELL_DEV, CELL_WIDTH)
    cot_all = cotangent.reshape(blocks, CELL_DEV, CELL_WIDTH)
    counts = cell_count.reshape(blocks).astype(jnp.int32)
    scale = 1.0 / float(SCEN * CELLS) ** 0.5

    def stats(item):
        input_rows, count = item
        next_value = front(input_rows, count, first_norm_gain, first_norm_bias, w_fx, w_x, w_slice, temper)
        return pool(next_value[6], next_value[3])
    slice_numerator, denom = lax.map(stats, (rows_all, counts))
    slice_numerator = slice_numerator.reshape(SCEN, SHARDS, ATTENTION_HEADS, SLICES, HEAD_SIZE).sum(axis=1)
    denom = denom.reshape(SCEN, SHARDS, ATTENTION_HEADS, SLICES).sum(axis=1)
    lifted = denom[..., None] + EPS
    slice_tokens = slice_numerator / lifted
    mixed = jax.vmap(mix_tokens, in_axes=(0, None, None, None))(slice_tokens, query_weight, key_weight, value_weight)
    mixed_token_batch = mixed.astype(jnp.bfloat16)
    mixed_rep = jnp.repeat(mixed_token_batch, SHARDS, axis=0)
    zero_late = (jnp.zeros((CELL_WIDTH, CELL_WIDTH), jnp.float32), jnp.zeros((CELL_WIDTH,), jnp.float32), jnp.zeros((CELL_WIDTH,), jnp.float32), jnp.zeros((CELL_WIDTH, CELL_WIDTH), jnp.float32), jnp.zeros((CELL_WIDTH, CELL_WIDTH), jnp.float32))

    def second(carry, item):
        input_rows, cot, count, mixed_one = item
        next_value = front(input_rows, count, first_norm_gain, first_norm_bias, w_fx, w_x, w_slice, temper)
        layer, residual_gradient, spread_gradient, token_partial, late = middle(input_rows, next_value[6], mixed_one, cot, w_out, second_norm_gain, second_norm_bias, w_up, w_down)
        carry = tuple((a + b for a, b in zip(carry, late)))
        return (carry, (layer, residual_gradient, spread_gradient, token_partial))
    late, (layer, g_resid_all, g_spread_all, tok_parts) = lax.scan(second, zero_late, (rows_all, cot_all, counts, mixed_rep))
    tok_grad = tok_parts.reshape(SCEN, SHARDS, ATTENTION_HEADS, SLICES, HEAD_SIZE).sum(axis=1)

    def back_mix(tok, grad_tok):
        unused, back = jax.vjp(mix_tokens, tok, query_weight, key_weight, value_weight)
        return back(grad_tok)
    g_tokens, grad_q, grad_k, grad_v = jax.vmap(back_mix)(slice_tokens, tok_grad)
    numerator_gradient = lax.optimization_barrier((g_tokens / lifted).astype(jnp.bfloat16))
    g_denom = -lax.optimization_barrier(jnp.sum(g_tokens * slice_tokens, axis=-1)) / lifted[..., 0]
    g_numer_rep = jnp.repeat(numerator_gradient, SHARDS, axis=0)
    g_denom_rep = jnp.repeat(g_denom, SHARDS, axis=0)
    zero_early = (jnp.zeros((CELL_WIDTH,), jnp.float32), jnp.zeros((CELL_WIDTH,), jnp.float32), jnp.zeros((CELL_WIDTH, CELL_WIDTH), jnp.float32), jnp.zeros((CELL_WIDTH, CELL_WIDTH), jnp.float32), jnp.zeros((HEAD_SIZE, SLICES), jnp.float32), jnp.zeros((ATTENTION_HEADS,), jnp.float32))

    def fourth(carry, item):
        input_rows, count, residual_gradient, spread_gradient, mixed_one, numer_one, denom_one = item
        next_value = front(input_rows, count, first_norm_gain, first_norm_bias, w_fx, w_x, w_slice, temper)
        row_gradient, early = rear(next_value, residual_gradient, spread_gradient, mixed_one, numer_one, denom_one, w_fx, w_x, w_slice, temper, first_norm_gain)
        carry = tuple((a + b for a, b in zip(carry, early)))
        return (carry, row_gradient)
    early, row_gradient = lax.scan(fourth, zero_early, (rows_all, counts, g_resid_all, g_spread_all, mixed_rep, g_numer_rep, g_denom_rep))
    grad_out, second_gain_gradient, grad_bias2, grad_up, grad_down = late
    first_gain_gradient, grad_bias1, grad_fx, grad_x, grad_slice, grad_temper = early
    return (layer.reshape(SCEN, CELLS, CELL_WIDTH), row_gradient.reshape(SCEN, CELLS, CELL_WIDTH), first_gain_gradient * scale, grad_bias1 * scale, grad_fx * scale, grad_x * scale, grad_slice * scale, grad_temper * scale, lax.optimization_barrier(jnp.sum(grad_q, axis=0)) * scale, lax.optimization_barrier(jnp.sum(grad_k, axis=0)) * scale, lax.optimization_barrier(jnp.sum(grad_v, axis=0)) * scale, grad_out * scale, second_gain_gradient * scale, grad_bias2 * scale, grad_up * scale, grad_down * scale)
```

```python
import math

import jax
import jax.numpy as jnp
from jax import lax
from jax.experimental import pallas as pl
from jax.experimental.pallas import tpu as pltpu
from jax.sharding import Mesh, PartitionSpec as P

WIDTH = 256
HEADS = 8
SLICES = 64
HEAD = 32
CELLS = 1024
PAIRS = HEADS // 2
EPS = 1e-05
CHUNK = 256
STEPS = CELLS // CHUNK
F32 = jnp.float32
BF16 = jnp.bfloat16
AXES = ("yl", "x", "yh", "z", "c")
PLANE = ("yl", "x", "yh")
SPACE = 32
Z_SCALE = 1.0 / math.sqrt(8 * 32768)
LATE, EARLY = 1536, 1280
LATE_HALF, EARLY_HALF = LATE // 2, EARLY // 2
LATE_PART, EARLY_PART = LATE_HALF // 16, EARLY_HALF // 16


def nn(a, b, precision=None):
    return lax.dot_general(
        a, b, (((1,), (0,)), ((), ())), precision=precision, preferred_element_type=F32
    )


def nt(a, b, precision=None):
    return lax.dot_general(
        a, b, (((1,), (1,)), ((), ())), precision=precision, preferred_element_type=F32
    )


def exact(f, a, b):
    return f(a, b, precision=lax.Precision.HIGHEST)


def turned(w):
    return w.astype(F32).T.astype(BF16)


def lane_half(rows):
    return lax.broadcasted_iota(jnp.int32, (rows, 128), 1) < SLICES


def diagonal_128():
    row = lax.broadcasted_iota(jnp.int32, (128, 128), 0) < SLICES
    lane = lax.broadcasted_iota(jnp.int32, (128, 128), 1) < SLICES
    return row == lane


def spread_pair(t):
    first = lane_half(HEAD)
    return jnp.concatenate([jnp.where(first, t, 0.0), jnp.where(first, 0.0, t)], axis=0)


def fold_pair(d):
    return jnp.where(lane_half(HEAD), d[:HEAD], d[HEAD:])


def slice_pair(w_slice):
    w = w_slice.astype(F32)
    return spread_pair(jnp.concatenate([w, w], axis=1))


def norm_stats(xt):
    mean = jnp.sum(xt, axis=0, keepdims=True) * (1.0 / WIDTH)
    centred = xt - mean
    inv = lax.rsqrt(jnp.sum(centred * centred, axis=0, keepdims=True) * (1.0 / WIDTH) + EPS)
    return mean, inv, centred * inv


def norm_back(g, xhat, inv, gain):
    ng = g * gain
    m1 = jnp.sum(ng, axis=0, keepdims=True) * (1.0 / WIDTH)
    m2 = jnp.sum(ng * xhat, axis=0, keepdims=True) * (1.0 / WIDTH)
    return inv * (ng - m1 - xhat * m2)


def lanes128(v):
    return v[:, :128] + v[:, 128:]


def live_row(count, step):
    lane = lax.broadcasted_iota(jnp.int32, (1, CHUNK), 1) + step * CHUNK
    return (lane < count).astype(F32)


def as_row(column128):
    return jnp.sum(column128.T, axis=0, keepdims=True)


def front_kernel(
    count_ref, temper_ref, cells_ref, gain_ref, bias_ref, wfx_ref, wx_ref, wsl_ref,
    pay_ref, xt_ref, feats_ref, mids_ref, weights_ref, stats_ref,
):
    count = count_ref[0]
    wfx_t = turned(wfx_ref[...])
    wx_t = turned(wx_ref[...])
    pair_t = slice_pair(wsl_ref[...]).T.astype(BF16)
    gain = gain_ref[...]
    bias = bias_ref[...]
    inv_t = [1.0 / jnp.full((1, CHUNK), temper_ref[h], F32) for h in range(HEADS)]
    ones = jnp.ones((16, CHUNK), BF16)
    pay_ref[...] = jnp.zeros_like(pay_ref)

    def step(i, carry):
        at = pl.ds(pl.multiple_of(i * CHUNK, CHUNK), CHUNK)
        xt = cells_ref[at, :].astype(F32).T
        xt_ref[:, at] = xt.astype(BF16)
        mean, inv, xhat = norm_stats(xt)
        n1 = (xhat * gain + bias).astype(BF16)
        feats = nn(wfx_t, n1).astype(BF16)
        mids = nn(wx_t, n1).astype(BF16)
        feats_ref[:, at] = feats
        mids_ref[:, at] = mids
        live = live_row(count, i)
        lses = []
        for p in range(PAIRS):
            rows = slice(64 * p, 64 * p + 64)
            logits = nn(pair_t, mids[rows])
            halves = []
            for k in range(2):
                l = logits[64 * k : 64 * k + 64] * inv_t[2 * p + k]
                m = jnp.max(l, axis=0, keepdims=True)
                e = jnp.exp(l - m)
                s = jnp.sum(e, axis=0, keepdims=True)
                halves.append((e * (live / s)).astype(BF16))
                lses.append(m + jnp.log(s))
            w = jnp.concatenate(halves, axis=0)
            weights_ref[128 * p : 128 * p + 128, at] = w
            d = nt(jnp.concatenate([feats[rows], ones], axis=0), w)
            part = jnp.concatenate([fold_pair(d[:64]), d[64:72]], axis=0)
            pay_ref[:, 128 * p : 128 * p + 128] += part
        stats_ref[:, at] = jnp.concatenate(
            [mean, inv] + lses + [jnp.zeros((6, CHUNK), F32)], axis=0
        )
        return carry

    lax.fori_loop(0, STEPS, step, 0)


def middle_kernel(
    core_ref, pay_ref, wq_ref, wk_ref, wv_ref, xt_ref, weights_ref, cot_ref, wout_ref, wup_ref,
    wdown_ref, gain_ref, bias_ref,
    layer_ref, gres_ref, gs_ref, tok_ref, keep_ref, send_ref, ln2_ref, mix_ref,
    late_ref, sums_ref,
):
    core = core_ref[0]
    lifted = pay_ref[HEAD : HEAD + 1, :] + EPS
    tok = pay_ref[:HEAD, :] / lifted
    qt = exact(nn, wq_ref[...].T, tok)
    kt = exact(nn, wk_ref[...].T, tok)
    vt = exact(nn, wv_ref[...].T, tok)
    mix_ref[0:32, :] = tok
    mix_ref[32:64, :] = qt
    mix_ref[64:96, :] = kt
    mix_ref[96:128, :] = vt
    diagonal = diagonal_128()
    blocks = []
    for p in range(PAIRS):
        lanes = slice(128 * p, 128 * p + 128)
        scores = exact(nn, kt[:, lanes].T, qt[:, lanes]) * (HEAD**-0.5)
        scores = jnp.where(diagonal, scores, -1e30)
        e = jnp.exp(scores - jnp.max(scores, axis=0, keepdims=True))
        e = jnp.where(diagonal, e, 0.0)
        attn = e / jnp.sum(e, axis=0, keepdims=True)
        mixed = exact(nn, vt[:, lanes], attn)
        mix_ref[128:256, lanes] = attn
        mixed_b = mixed.astype(BF16).astype(F32)
        mix_ref[256:288, lanes] = mixed_b
        blocks.append(spread_pair(mixed_b).astype(BF16))

    wout = wout_ref[...]
    wup = wup_ref[...]
    wdown = wdown_ref[...]
    wout_t, wup_t, wdown_t = turned(wout), turned(wup), turned(wdown)
    gain = gain_ref[...]
    bias = bias_ref[...]
    late_ref[...] = jnp.zeros_like(late_ref)
    sums_ref[...] = jnp.zeros_like(sums_ref)
    tok_ref[...] = jnp.zeros_like(tok_ref)
    c0 = math.sqrt(2.0 / math.pi)

    def step(i, carry):
        at = pl.ds(pl.multiple_of(i * CHUNK, CHUNK), CHUNK)
        spread = jnp.concatenate(
            [nn(blocks[p], weights_ref[128 * p : 128 * p + 128, at]) for p in range(PAIRS)], axis=0
        ).astype(BF16)
        resid = (xt_ref[:, at].astype(F32) + nn(wout_t, spread)).astype(BF16)
        resid_f = resid.astype(F32)
        _, inv, xhat = norm_stats(resid_f)
        n2 = (xhat * gain + bias).astype(BF16)
        up = nn(wup_t, n2)
        sq = up * up
        t = jnp.tanh(c0 * up * (1.0 + 0.044715 * sq))
        half = 0.5 * (1.0 + t)
        act = (up * half).astype(BF16)
        slope = half + 0.5 * up * (1.0 - t * t) * (c0 * (1.0 + 3.0 * 0.044715 * sq))
        layer = (resid_f + nn(wdown_t, act)).astype(BF16)
        layer_ref[at, :] = layer.astype(F32).T.astype(BF16)
        gt_f = cot_ref[at, :].astype(F32).T
        gt = gt_f.astype(BF16)
        late_ref[512:768, :] += nt(act, gt)
        g_up = (slope * nn(wdown, gt)).astype(BF16)
        late_ref[256:512, :] += nt(n2, g_up)
        g_n2 = nn(wup, g_up)
        sums_ref[0:256, :] += lanes128(g_n2 * xhat)
        sums_ref[256:512, :] += lanes128(g_n2)
        gres = gt_f + norm_back(g_n2, xhat, inv, gain)
        gres_ref[:, at] = gres
        gres_b = gres.astype(BF16)
        late_ref[0:256, :] += nt(spread, gres_b)
        gs = nn(wout, gres_b).astype(BF16)
        gs_ref[:, at] = gs
        for p in range(PAIRS):
            d = nt(gs[64 * p : 64 * p + 64], weights_ref[128 * p : 128 * p + 128, at])
            tok_ref[:, 128 * p : 128 * p + 128] += fold_pair(d)
        return carry

    lax.fori_loop(0, STEPS, step, 0)
    left = late_ref[:, :128] * Z_SCALE
    right = late_ref[:, 128:] * Z_SCALE
    keep_ref[...] = jnp.where(core == 0, left, right)
    send_ref[...] = jnp.where(core == 0, right, left)
    ln2_ref[...] = jnp.concatenate(
        [as_row(sums_ref[0:256, :]), as_row(sums_ref[256:512, :]), jnp.zeros((6, WIDTH), F32)],
        axis=0,
    )


def rear_kernel(
    core_ref, count_ref, temper_ref, pay_ref, grad_ref, mix_ref, wq_ref, wk_ref, wv_ref, xt_ref,
    feats_ref, mids_ref, stats_ref, gs_ref, gres_ref, gain_ref, bias_ref, wfx_ref, wx_ref,
    wsl_ref, ln2_ref,
    cells_out_ref, keep_ref, send_ref,
    early_ref, sums_ref, small_ref, temp_ref,
):
    core = core_ref[0]
    count = count_ref[0]
    lifted = pay_ref[HEAD : HEAD + 1, :] + EPS
    tok = mix_ref[0:32, :]
    qt = mix_ref[32:64, :]
    kt = mix_ref[64:96, :]
    vt = mix_ref[96:128, :]
    dqs, dks, dvs = [], [], []
    for p in range(PAIRS):
        lanes = slice(128 * p, 128 * p + 128)
        gm = grad_ref[:, lanes]
        attn = mix_ref[128:256, lanes]
        da = exact(nn, vt[:, lanes].T, gm)
        dvs.append(exact(nt, gm, attn))
        pulled = attn * da
        ds = (pulled - attn * jnp.sum(pulled, axis=0, keepdims=True)) * (HEAD**-0.5)
        dqs.append(exact(nn, kt[:, lanes], ds))
        dks.append(exact(nt, qt[:, lanes], ds))
    dq = jnp.concatenate(dqs, axis=1)
    dk = jnp.concatenate(dks, axis=1)
    dv = jnp.concatenate(dvs, axis=1)
    dtok = exact(nn, wq_ref[...], dq) + exact(nn, wk_ref[...], dk) + exact(nn, wv_ref[...], dv)
    qkv = exact(nt, tok, jnp.concatenate([dq, dk, dv, jnp.zeros_like(dq)], axis=0))
    gnum = (dtok / lifted).astype(BF16).astype(F32)
    gden = -jnp.sum(dtok * tok, axis=0, keepdims=True) / lifted
    back_blocks, num_blocks, den_columns = [], [], []
    for p in range(PAIRS):
        lanes = slice(128 * p, 128 * p + 128)
        num = spread_pair(gnum[:, lanes])
        num_blocks.append(num.astype(BF16))
        both = jnp.concatenate([spread_pair(mix_ref[256:288, lanes]), num], axis=0)
        back_blocks.append(both.T.astype(BF16))
        den_columns.append(jnp.broadcast_to(gden[:, lanes], (128, 128)).T[:, 0:1])

    pair = slice_pair(wsl_ref[...])
    pair_b = pair.astype(BF16)
    pair_t = pair.T.astype(BF16)
    wfx = wfx_ref[...]
    wx = wx_ref[...]
    gain = gain_ref[...]
    bias = bias_ref[...]
    inv_t = [1.0 / jnp.full((1, CHUNK), temper_ref[h], F32) for h in range(HEADS)]
    early_ref[...] = jnp.zeros_like(early_ref)
    sums_ref[...] = jnp.zeros_like(sums_ref)
    small_ref[...] = jnp.zeros_like(small_ref)
    temp_ref[...] = jnp.zeros_like(temp_ref)

    def step(i, carry):
        at = pl.ds(pl.multiple_of(i * CHUNK, CHUNK), CHUNK)
        live = live_row(count, i)
        stats = stats_ref[:, at]
        mean, inv = stats[0:1], stats[1:2]
        g_mids, g_feats, temps = [], [], []
        for p in range(PAIRS):
            rows = slice(64 * p, 64 * p + 64)
            mids = mids_ref[rows, at]
            logits = nn(pair_t, mids)
            gw = nn(
                back_blocks[p], jnp.concatenate([gs_ref[rows, at], feats_ref[rows, at]], axis=0)
            )
            gw = gw + den_columns[p]
            scaled, weights = [], []
            for k in range(2):
                h = 2 * p + k
                part = slice(64 * k, 64 * k + 64)
                l = logits[part] * inv_t[h]
                pr = jnp.exp(l - stats[2 + h : 3 + h]) * live
                weights.append(pr.astype(BF16))
                g = gw[part]
                pulled = g * pr
                gl = pulled - pr * jnp.sum(pulled, axis=0, keepdims=True)
                temps.append(jnp.sum(gl * l, axis=0, keepdims=True))
                scaled.append((gl * inv_t[h]).astype(BF16))
            scaled = jnp.concatenate(scaled, axis=0)
            g_mids.append(nn(pair_b, scaled))
            small_ref[:, 0:128] += fold_pair(nt(mids, scaled))
            g_feats.append(nn(num_blocks[p], jnp.concatenate(weights, axis=0)))
        temp_ref[...] += lanes128(jnp.concatenate(temps, axis=0))
        g_mids = jnp.concatenate(g_mids, axis=0).astype(BF16)
        g_feats = jnp.concatenate(g_feats, axis=0).astype(BF16)
        xhat = (xt_ref[:, at].astype(F32) - mean) * inv
        n1 = (xhat * gain + bias).astype(BF16)
        early_ref[0:256, :] += nt(n1, g_feats)
        early_ref[256:512, :] += nt(n1, g_mids)
        g_n1 = nn(wfx, g_feats) + nn(wx, g_mids)
        sums_ref[0:256, :] += lanes128(g_n1 * xhat)
        sums_ref[256:512, :] += lanes128(g_n1)
        out = gres_ref[:, at] + norm_back(g_n1, xhat, inv, gain)
        cells_out_ref[at, :] = out.T.astype(BF16)
        return carry

    lax.fori_loop(0, STEPS, step, 0)
    slices = small_ref[:, 0:128]
    slices = slices + pltpu.roll(slices, 64, 1)
    inv_col = jnp.concatenate([t[:, :128] for t in inv_t], axis=0)
    temper = -jnp.broadcast_to(jnp.sum(temp_ref[...], axis=1, keepdims=True), (8, 128)) * inv_col
    rows = jnp.concatenate(
        [as_row(sums_ref[0:256, :]), as_row(sums_ref[256:512, :]), ln2_ref[0:2, :],
         jnp.zeros((4, WIDTH), F32)],
        axis=0,
    )
    zeros = jnp.zeros((EARLY_HALF - 560, 128), F32)
    left = jnp.concatenate([early_ref[:, :128], slices, temper, rows[:, :128], zeros], axis=0)
    right = jnp.concatenate(
        [early_ref[:, 128:], qkv * (1.0 / SPACE), jnp.zeros((8, 128), F32), rows[:, 128:], zeros],
        axis=0,
    )
    left = left * Z_SCALE
    right = right * Z_SCALE
    keep_ref[...] = jnp.where(core == 0, left, right)
    send_ref[...] = jnp.where(core == 0, right, left)


def last_kernel(
    core_ref, mine_ref, theirs_ref,
    fx_ref, x_ref, out_ref, up_ref, down_ref, slice_ref, q_ref, k_ref, v_ref, temper_ref, rows_ref,
    whole_ref,
):
    core = core_ref[0]
    for part in range(16):
        mine = mine_ref[part]
        theirs = theirs_ref[part]
        left = jnp.where(core == 0, mine, theirs)
        right = jnp.where(core == 0, theirs, mine)
        both = jnp.concatenate([left, right], axis=1)
        whole_ref[part * LATE_PART : (part + 1) * LATE_PART, :] = both[:LATE_PART]
        at = LATE_HALF + part * EARLY_PART
        whole_ref[at : at + EARLY_PART, :] = both[LATE_PART:]
    out_ref[...] = whole_ref[0:256, :]
    up_ref[...] = whole_ref[256:512, :]
    down_ref[...] = whole_ref[512:768, :]
    fx_ref[...] = whole_ref[768:1024, :]
    x_ref[...] = whole_ref[1024:1280, :]
    slice_ref[...] = whole_ref[1280:1312, 0:64]
    qkv = whole_ref[1280:1312, 128:256]
    q_ref[...] = qkv[:, 0:32]
    k_ref[...] = qkv[:, 32:64]
    v_ref[...] = qkv[:, 64:96]
    temper_ref[...] = whole_ref[1312:1320, 0:128]
    rows_ref[...] = whole_ref[1320:1328, :]


def permutation(move):
    pairs = []
    for yl in range(2):
        for x in range(4):
            for yh in range(2):
                for z in range(8):
                    for c in range(2):
                        place = lambda a, b, e, f, g: (((a * 4 + b) * 2 + e) * 8 + f) * 2 + g
                        pairs.append((place(yl, x, yh, z, c), place(*move(yl, x, yh, z, c))))
    return pairs


OTHER_CORE = permutation(lambda yl, x, yh, z, c: (yl, x, yh, z, 1 - c))
Z_ONE = permutation(lambda yl, x, yh, z, c: (yl, x, yh, z ^ 1, c))
Z_TWO = permutation(lambda yl, x, yh, z, c: (yl, x, yh, z ^ 2, c))
Z_FAR = permutation(lambda yl, x, yh, z, c: (yl, x, yh, 7 - z, c))
Y_FAR = permutation(lambda yl, x, yh, z, c: (yl, x, 1 - yh, z, c))


def swap(v, pairs):
    return lax.ppermute(v, AXES, pairs)


def space_sum(v):
    for pairs in (OTHER_CORE, Z_ONE, Z_TWO, Z_FAR, Y_FAR):
        v = v + swap(v, pairs)
    return v


VMEM = pl.BlockSpec(memory_space=pltpu.VMEM)
SMEM = pl.BlockSpec(memory_space=pltpu.SMEM)
PARAMS = pltpu.CompilerParams(vmem_limit_bytes=40 * 1024 * 1024)


def call(kernel, name, outs, scalars, arrays, scratch=()):
    return pl.pallas_call(
        kernel,
        name=name,
        out_shape=[jax.ShapeDtypeStruct(shape, dtype) for shape, dtype in outs],
        in_specs=[SMEM] * len(scalars) + [VMEM] * len(arrays),
        out_specs=[VMEM] * len(outs),
        scratch_shapes=[pltpu.VMEM(shape, F32) for shape in scratch],
        compiler_params=PARAMS,
    )(*scalars, *arrays)


def body(
    cells, cotangent, cell_count, first_norm_gain, first_norm_bias, w_fx, w_x, w_slice, temper,
    query_weight, key_weight, value_weight, w_out, second_norm_gain, second_norm_bias, w_up, w_down,
):
    rows, cot = cells[0], cotangent[0]
    count = cell_count.reshape(1)
    core = lax.axis_index("c").astype(jnp.int32).reshape(1)
    gain1, bias1 = first_norm_gain.reshape(WIDTH, 1), first_norm_bias.reshape(WIDTH, 1)
    gain2, bias2 = second_norm_gain.reshape(WIDTH, 1), second_norm_bias.reshape(WIDTH, 1)
    pay, xt, feats, mids, weights, stats = call(
        front_kernel, "front",
        [((40, 512), F32), ((WIDTH, CELLS), BF16), ((WIDTH, CELLS), BF16), ((WIDTH, CELLS), BF16),
         ((512, CELLS), BF16), ((16, CELLS), F32)],
        [count, temper], [rows, gain1, bias1, w_fx, w_x, w_slice],
    )
    pay = space_sum(pay)
    layer, gres, gs, tok, keep2, send2, ln2, mix = call(
        middle_kernel, "middle",
        [((CELLS, WIDTH), BF16), ((WIDTH, CELLS), F32), ((WIDTH, CELLS), BF16), ((HEAD, 512), F32),
         ((LATE_HALF, 128), F32), ((LATE_HALF, 128), F32), ((8, WIDTH), F32), ((288, 512), F32)],
        [core],
        [pay, query_weight, key_weight, value_weight, xt, weights, cot, w_out, w_up, w_down, gain2,
         bias2],
        [(768, WIDTH), (512, 128)],
    )
    tok = space_sum(tok)
    late = keep2 + swap(send2, OTHER_CORE)
    out_rows, keep3, send3 = call(
        rear_kernel, "rear",
        [((CELLS, WIDTH), BF16), ((EARLY_HALF, 128), F32), ((EARLY_HALF, 128), F32)],
        [core, count, temper],
        [pay, tok, mix, query_weight, key_weight, value_weight, xt, feats, mids, stats, gs, gres,
         gain1, bias1, w_fx, w_x, w_slice, ln2],
        [(512, WIDTH), (512, 128), (HEAD, 128), (8, 128)],
    )
    early = keep3 + swap(send3, OTHER_CORE)
    both = jnp.concatenate(
        [late.reshape(16, LATE_PART, 128), early.reshape(16, EARLY_PART, 128)], axis=1
    )
    part = jnp.sum(lax.all_to_all(both, PLANE, 0, 0), axis=0)
    for pairs in (Z_ONE, Z_TWO, Z_FAR):
        part = part + swap(part, pairs)
    mine = lax.all_to_all(jnp.broadcast_to(part[None], both.shape), PLANE, 0, 0)
    theirs = swap(mine, OTHER_CORE)
    fx, gx, out, up, down, sl, q, k, v, temp, norms = call(
        last_kernel, "last",
        [((WIDTH, WIDTH), F32)] * 5
        + [((HEAD, SLICES), F32)] + [((HEAD, HEAD), F32)] * 3 + [((8, 128), F32), ((8, WIDTH), F32)],
        [core], [mine, theirs],
        [(LATE_HALF + EARLY_HALF, WIDTH)],
    )
    return (
        layer[None], out_rows[None], norms[0], norms[1], fx, gx, sl, temp[:, 0], q, k, v, out,
        norms[2], norms[3], up, down,
    )


def solution(mesh):
    fine = Mesh(mesh.devices.reshape(2, 4, 2, 8, 2), AXES)
    split = P(("yl", "x"), ("yh", "z", "c"), None)
    return jax.shard_map(
        body,
        mesh=fine,
        in_specs=(split, split, P(("yl", "x"), ("yh", "z", "c"))) + (P(),) * 14,
        out_specs=(split, split) + (P(),) * 14,
        check_vma=False,
    )
```

```python
import math

import jax
import jax.numpy as jnp
from jax import lax
from jax.experimental import pallas as pl
from jax.experimental.pallas import tpu as pltpu
from jax.sharding import Mesh, PartitionSpec as P

WIDTH = 256
HEADS = 8
SLICES = 64
HEAD = 32
CELLS = 1024
PAIRS = HEADS // 2
EPS = 1e-05
F32 = jnp.float32
BF16 = jnp.bfloat16
AXES = ("yl", "x", "yh", "z", "c")
PLANE = ("yl", "x", "yh")
SPACE = 32
Z_SCALE = 1.0 / math.sqrt(8 * 32768)
LATE, EARLY = 1536, 1280
LATE_HALF, EARLY_HALF = LATE // 2, EARLY // 2
LATE_PART, EARLY_PART = LATE_HALF // 16, EARLY_HALF // 16


def nn(a, b, precision=None):
    return lax.dot_general(
        a, b, (((1,), (0,)), ((), ())), precision=precision, preferred_element_type=F32
    )


def nt(a, b, precision=None):
    return lax.dot_general(
        a, b, (((1,), (1,)), ((), ())), precision=precision, preferred_element_type=F32
    )


def exact(f, a, b):
    return f(a, b, precision=lax.Precision.HIGHEST)


def turned(w):
    return w.astype(F32).T.astype(BF16)


def lane_half(rows):
    return lax.broadcasted_iota(jnp.int32, (rows, 128), 1) < SLICES


def diagonal_128():
    row = lax.broadcasted_iota(jnp.int32, (128, 128), 0) < SLICES
    lane = lax.broadcasted_iota(jnp.int32, (128, 128), 1) < SLICES
    return row == lane


def spread_pair(t):
    first = lane_half(HEAD)
    return jnp.concatenate([jnp.where(first, t, 0.0), jnp.where(first, 0.0, t)], axis=0)


def fold_pair(d):
    return jnp.where(lane_half(HEAD), d[:HEAD], d[HEAD:])


def slice_pair(w_slice):
    w = w_slice.astype(F32)
    return spread_pair(jnp.concatenate([w, w], axis=1))


def norm_stats(xt):
    mean = jnp.sum(xt, axis=0, keepdims=True) * (1.0 / WIDTH)
    centred = xt - mean
    inv = lax.rsqrt(jnp.sum(centred * centred, axis=0, keepdims=True) * (1.0 / WIDTH) + EPS)
    return mean, inv, centred * inv


def norm_back(g, xhat, inv, gain):
    ng = g * gain
    m1 = jnp.sum(ng, axis=0, keepdims=True) * (1.0 / WIDTH)
    m2 = jnp.sum(ng * xhat, axis=0, keepdims=True) * (1.0 / WIDTH)
    return inv * (ng - m1 - xhat * m2)


def lanes128(v):
    return sum(v[:, i : i + 128] for i in range(128, CELLS, 128)) + v[:, :128]


def live_row(count):
    return (lax.broadcasted_iota(jnp.int32, (1, CELLS), 1) < count).astype(F32)


def as_row(column128):
    return jnp.sum(column128.T, axis=0, keepdims=True)


def as_column(row):
    return jnp.broadcast_to(row, (128, row.shape[1])).T[:, 0:1]


def inverse_temper(temper_ref):
    return [1.0 / jnp.full((1, CELLS), temper_ref[h], F32) for h in range(HEADS)]


def fetch(sources, targets, sems):
    copies = [
        pltpu.make_async_copy(source, target, sems.at[i])
        for i, (source, target) in enumerate(zip(sources, targets))
    ]
    for copy in copies:
        copy.start()
    return copies


def front_kernel(
    count_ref, temper_hbm, cells_hbm, gain_hbm, bias_hbm, wfx_hbm, wx_hbm, wsl_hbm, gain2_hbm,
    bias2_hbm,
    pay_ref, feats_ref, mids_ref, weights_ref, stats_ref,
    temper_ref, cells_ref, gain_ref, bias_ref, wfx_ref, wx_ref, wsl_ref, gain2_ref, bias2_ref, sems,
):
    copies = fetch(
        (cells_hbm, wx_hbm, wsl_hbm, gain_hbm, bias_hbm, wfx_hbm, temper_hbm, gain2_hbm, bias2_hbm),
        (cells_ref, wx_ref, wsl_ref, gain_ref, bias_ref, wfx_ref, temper_ref, gain2_ref, bias2_ref),
        sems,
    )
    ones = jnp.ones((16, CELLS), BF16)
    for copy in copies:
        copy.wait()
    pair_t = slice_pair(wsl_ref[...]).T.astype(BF16)
    inv_t = inverse_temper(temper_ref)
    xt = cells_ref[...].astype(F32).T
    mean, inv, xhat = norm_stats(xt)
    n1 = (xhat * as_column(gain_ref[...]) + as_column(bias_ref[...])).astype(BF16)
    mids = nn(turned(wx_ref[...]), n1).astype(BF16)
    feats = nn(turned(wfx_ref[...]), n1).astype(BF16)
    mids_ref[...] = mids
    feats_ref[...] = feats
    live = live_row(count_ref[0, 0])
    stats_ref[14:15, :] = live
    stats_ref[0:1, :] = mean
    stats_ref[1:2, :] = inv
    for i, ref in enumerate((gain_ref, bias_ref, gain2_ref, bias2_ref)):
        stats_ref[10 + i : 11 + i, 0:WIDTH] = ref[...]
    for p in range(PAIRS):
        rows = slice(64 * p, 64 * p + 64)
        logits = nn(pair_t, mids[rows])
        halves = []
        for k in range(2):
            h = 2 * p + k
            l = logits[64 * k : 64 * k + 64] * inv_t[h]
            m = jnp.max(l, axis=0, keepdims=True)
            e = jnp.exp(l - m)
            s = jnp.sum(e, axis=0, keepdims=True)
            halves.append((e * (live / s)).astype(BF16))
            stats_ref[2 + h : 3 + h, :] = m + jnp.log(s)
        w = jnp.concatenate(halves, axis=0)
        weights_ref[128 * p : 128 * p + 128, :] = w
        d = nt(jnp.concatenate([feats[rows], ones], axis=0), w)
        pay_ref[0:32, 128 * p : 128 * p + 128] = fold_pair(d[:64])
        pay_ref[32:40, 128 * p : 128 * p + 128] = d[64:72]


def middle_kernel(
    core_ref, pay_ref, wq_ref, wk_ref, wv_ref, weights_ref, stats_ref, cells_ref, cot_ref, wout_ref,
    wup_ref, wdown_ref,
    tok_ref, gres_ref, gs_ref, keep_ref, send_ref, ln2_ref, mix_ref, xt_ref, layer_hbm,
    layer_ref, sems,
):
    core = core_ref[0]
    lifted = pay_ref[HEAD : HEAD + 1, :] + EPS
    tok = pay_ref[:HEAD, :] / lifted
    qt = exact(nn, wq_ref[...].T, tok)
    kt = exact(nn, wk_ref[...].T, tok)
    vt = exact(nn, wv_ref[...].T, tok)
    mix_ref[0:32, :] = tok
    mix_ref[32:64, :] = qt
    mix_ref[64:96, :] = kt
    mix_ref[96:128, :] = vt
    mix_ref[288:296, :] = jnp.broadcast_to(lifted, (8, 512))
    diagonal = diagonal_128()

    def give(at, grad):
        left = grad[:, :128] * Z_SCALE
        right = grad[:, 128:] * Z_SCALE
        keep_ref[at : at + 256, :] = jnp.where(core == 0, left, right)
        send_ref[at : at + 256, :] = jnp.where(core == 0, right, left)

    spread = []
    for p in range(PAIRS):
        lanes = slice(128 * p, 128 * p + 128)
        scores = exact(nn, kt[:, lanes].T, qt[:, lanes]) * (HEAD**-0.5)
        scores = jnp.where(diagonal, scores, -1e30)
        e = jnp.exp(scores - jnp.max(scores, axis=0, keepdims=True))
        e = jnp.where(diagonal, e, 0.0)
        attn = e / jnp.sum(e, axis=0, keepdims=True)
        mixed = exact(nn, vt[:, lanes], attn)
        mix_ref[128:256, lanes] = attn
        mixed = mixed.astype(BF16).astype(F32)
        mix_ref[256:288, lanes] = mixed
        spread.append(
            nn(spread_pair(mixed).astype(BF16), weights_ref[128 * p : 128 * p + 128, :])
        )
    xt = cells_ref[...].astype(F32).T
    xt_ref[...] = xt.astype(BF16)
    gain = as_column(stats_ref[12:13, 0:WIDTH])
    bias = as_column(stats_ref[13:14, 0:WIDTH])
    c0 = math.sqrt(2.0 / math.pi)
    gt = cot_ref[...].astype(F32).T.astype(BF16)
    g_act = nn(wdown_ref[...], gt)
    spread = jnp.concatenate(spread, axis=0).astype(BF16)
    resid = (xt + nn(turned(wout_ref[...]), spread)).astype(BF16)
    _, inv, xhat = norm_stats(resid.astype(F32))
    n2 = (xhat * gain + bias).astype(BF16)
    up = nn(turned(wup_ref[...]), n2)
    sq = up * up
    t = jnp.tanh(c0 * up * (1.0 + 0.044715 * sq))
    half = 0.5 * (1.0 + t)
    act = (up * half).astype(BF16)
    layer = resid.astype(F32) + nn(turned(wdown_ref[...]), act)
    layer_ref[...] = layer.T.astype(BF16)
    (leave,) = fetch((layer_ref,), (layer_hbm,), sems)
    give(512, nt(act, gt))
    slope = half + 0.5 * up * (1.0 - t * t) * (c0 * (1.0 + 3.0 * 0.044715 * sq))
    g_up = (slope * g_act).astype(BF16)
    give(256, nt(n2, g_up))
    g_n2 = nn(wup_ref[...], g_up)
    ln2_ref[0:1, :] = as_row(lanes128(g_n2 * xhat))
    ln2_ref[1:2, :] = as_row(lanes128(g_n2))
    gres = gt.astype(F32) + norm_back(g_n2, xhat, inv, gain)
    gres_ref[...] = gres
    gres_b = gres.astype(BF16)
    give(0, nt(spread, gres_b))
    gs = nn(wout_ref[...], gres_b).astype(BF16)
    gs_ref[...] = gs
    for p in range(PAIRS):
        d = nt(gs[64 * p : 64 * p + 64], weights_ref[128 * p : 128 * p + 128, :])
        tok_ref[:, 128 * p : 128 * p + 128] = fold_pair(d)
    leave.wait()


def rear_kernel(
    core_ref, temper_ref, grad_ref, mix_ref, wq_ref, wk_ref, wv_ref, feats_ref, mids_ref,
    gs_ref, weights_ref, xt_ref, stats_ref, gres_ref, ln2_ref, wfx_ref, wx_ref, wsl_ref,
    keep_ref, send_ref, out_ref,
):
    core = core_ref[0]
    lifted = mix_ref[288:289, :]
    tok = mix_ref[0:32, :]
    qt = mix_ref[32:64, :]
    kt = mix_ref[64:96, :]
    vt = mix_ref[96:128, :]
    dqs, dks, dvs = [], [], []
    for p in range(PAIRS):
        lanes = slice(128 * p, 128 * p + 128)
        gm = grad_ref[:, lanes]
        attn = mix_ref[128:256, lanes]
        da = exact(nn, vt[:, lanes].T, gm)
        dvs.append(exact(nt, gm, attn))
        pulled = attn * da
        ds = (pulled - attn * jnp.sum(pulled, axis=0, keepdims=True)) * (HEAD**-0.5)
        dqs.append(exact(nn, kt[:, lanes], ds))
        dks.append(exact(nt, qt[:, lanes], ds))
    dq = jnp.concatenate(dqs, axis=1)
    dk = jnp.concatenate(dks, axis=1)
    dv = jnp.concatenate(dvs, axis=1)
    dtok = exact(nn, wq_ref[...], dq) + exact(nn, wk_ref[...], dk) + exact(nn, wv_ref[...], dv)
    qkv = exact(nt, tok, jnp.concatenate([dq, dk, dv, jnp.zeros_like(dq)], axis=0))
    gnum = (dtok / lifted).astype(BF16).astype(F32)
    gden = -jnp.sum(dtok * tok, axis=0, keepdims=True) / lifted

    live = stats_ref[14:15, :]
    pair_t = slice_pair(wsl_ref[...]).T.astype(BF16)
    pair_b = slice_pair(wsl_ref[...]).astype(BF16)
    inv_t = inverse_temper(temper_ref)
    g_mids, g_feats, temps, slices = [], [], [], 0.0
    for p in range(PAIRS):
        lanes = slice(128 * p, 128 * p + 128)
        rows = slice(64 * p, 64 * p + 64)
        num = spread_pair(gnum[:, lanes])
        g_feats.append(nn(num.astype(BF16), weights_ref[lanes, :]))
        both = jnp.concatenate([spread_pair(mix_ref[256:288, lanes]), num], axis=0)
        gw = nn(
            both.T.astype(BF16), jnp.concatenate([gs_ref[rows, :], feats_ref[rows, :]], axis=0)
        )
        den = as_column(gden[:, lanes])
        logits = nn(pair_t, mids_ref[rows, :])
        scaled = []
        for k in range(2):
            h = 2 * p + k
            part = slice(64 * k, 64 * k + 64)
            l = logits[part] * inv_t[h]
            pr = jnp.exp(l - stats_ref[2 + h : 3 + h, :]) * live
            pulled = (gw[part] + den[part]) * pr
            gl = pulled - pr * jnp.sum(pulled, axis=0, keepdims=True)
            temps.append(jnp.sum(gl * l, axis=0, keepdims=True))
            scaled.append((gl * inv_t[h]).astype(BF16))
        scaled = jnp.concatenate(scaled, axis=0)
        g_mids.append(nn(pair_b, scaled))
        slices = slices + fold_pair(nt(mids_ref[rows, :], scaled))
    g_mids = jnp.concatenate(g_mids, axis=0).astype(BF16)
    g_feats = jnp.concatenate(g_feats, axis=0).astype(BF16)
    gain = as_column(stats_ref[10:11, 0:WIDTH])
    inv = stats_ref[1:2, :]
    xhat = (xt_ref[...].astype(F32) - stats_ref[0:1, :]) * inv
    n1 = (xhat * gain + as_column(stats_ref[11:12, 0:WIDTH])).astype(BF16)
    grad_fx = nt(n1, g_feats)
    grad_x = nt(n1, g_mids)
    g_n1 = nn(wfx_ref[...], g_feats) + nn(wx_ref[...], g_mids)
    slices = slices + pltpu.roll(slices, 64, 1)
    inv_col = jnp.concatenate([t[:, :128] for t in inv_t], axis=0)
    temps = jnp.sum(lanes128(jnp.concatenate(temps, axis=0)), axis=1, keepdims=True)
    temper = -jnp.broadcast_to(temps, (8, 128)) * inv_col
    rows = jnp.concatenate(
        [as_row(lanes128(g_n1 * xhat)), as_row(lanes128(g_n1)), ln2_ref[0:2, :],
         jnp.zeros((4, WIDTH), F32)],
        axis=0,
    )

    def give(at, left, right):
        left = left * Z_SCALE
        right = right * Z_SCALE
        keep_ref[at : at + left.shape[0], :] = jnp.where(core == 0, left, right)
        send_ref[at : at + left.shape[0], :] = jnp.where(core == 0, right, left)

    give(0, grad_fx[:, :128], grad_fx[:, 128:])
    give(256, grad_x[:, :128], grad_x[:, 128:])
    give(512, slices, qkv * (1.0 / SPACE))
    give(544, temper, jnp.zeros((8, 128), F32))
    give(552, rows[:, :128], rows[:, 128:])
    nothing = jnp.zeros((EARLY_HALF - 560, 128), F32)
    give(560, nothing, nothing)
    out_ref[...] = (gres_ref[...] + norm_back(g_n1, xhat, inv, gain)).T.astype(BF16)


def last_kernel(
    core_ref, mine_ref, theirs_ref,
    fx_ref, x_ref, out_ref, up_ref, down_ref, slice_ref, q_ref, k_ref, v_ref, temper_ref, gain1_ref, bias1_ref,
    gain2_ref, bias2_ref,
    whole_ref,
):
    core = core_ref[0]
    for part in range(16):
        mine = mine_ref[part]
        theirs = theirs_ref[part]
        left = jnp.where(core == 0, mine, theirs)
        right = jnp.where(core == 0, theirs, mine)
        both = jnp.concatenate([left, right], axis=1)
        whole_ref[part * LATE_PART : (part + 1) * LATE_PART, :] = both[:LATE_PART]
        at = LATE_HALF + part * EARLY_PART
        whole_ref[at : at + EARLY_PART, :] = both[LATE_PART:]
    out_ref[...] = whole_ref[0:256, :]
    up_ref[...] = whole_ref[256:512, :]
    down_ref[...] = whole_ref[512:768, :]
    fx_ref[...] = whole_ref[768:1024, :]
    x_ref[...] = whole_ref[1024:1280, :]
    slice_ref[...] = whole_ref[1280:1312, 0:64]
    qkv = whole_ref[1280:1312, 128:256]
    q_ref[...] = qkv[:, 0:32]
    k_ref[...] = qkv[:, 32:64]
    v_ref[...] = qkv[:, 64:96]
    temper_ref[...] = whole_ref[1312:1320, 0:128].T[0:1, :]
    gain1_ref[...] = whole_ref[1320:1321, :]
    bias1_ref[...] = whole_ref[1321:1322, :]
    gain2_ref[...] = whole_ref[1322:1323, :]
    bias2_ref[...] = whole_ref[1323:1324, :]


def permutation(move):
    pairs = []
    for yl in range(2):
        for x in range(4):
            for yh in range(2):
                for z in range(8):
                    for c in range(2):
                        place = lambda a, b, e, f, g: (((a * 4 + b) * 2 + e) * 8 + f) * 2 + g
                        pairs.append((place(yl, x, yh, z, c), place(*move(yl, x, yh, z, c))))
    return pairs


OTHER_CORE = permutation(lambda yl, x, yh, z, c: (yl, x, yh, z, 1 - c))
Z_ONE = permutation(lambda yl, x, yh, z, c: (yl, x, yh, z ^ 1, c))
Z_TWO = permutation(lambda yl, x, yh, z, c: (yl, x, yh, z ^ 2, c))
Z_FAR = permutation(lambda yl, x, yh, z, c: (yl, x, yh, 7 - z, c))
Y_FAR = permutation(lambda yl, x, yh, z, c: (yl, x, 1 - yh, z, c))


def swap(v, pairs):
    return lax.ppermute(v, AXES, pairs)


def space_sum(v):
    for pairs in (OTHER_CORE, Z_ONE, Z_TWO, Z_FAR, Y_FAR):
        v = v + swap(v, pairs)
    return v


VMEM = pl.BlockSpec(memory_space=pltpu.VMEM)
SMEM = pl.BlockSpec(memory_space=pltpu.SMEM)
HBM = pl.BlockSpec(memory_space=pltpu.HBM)
PARAMS = pltpu.CompilerParams(vmem_limit_bytes=16 * 1024 * 1024)


def call(kernel, name, outs, scalars, held, fetched=(), scratch=(), left=0, copies=0):
    near = len(outs) - left
    fetched = [pltpu.with_memory_space_constraint(a, pltpu.HBM) for a in fetched]
    return pl.pallas_call(
        kernel,
        name=name,
        out_shape=[jax.ShapeDtypeStruct(shape, dtype) for shape, dtype in outs],
        in_specs=[SMEM] * len(scalars) + [VMEM] * len(held) + [HBM] * len(fetched),
        out_specs=[VMEM] * near + [HBM] * left,
        scratch_shapes=list(scratch) + [pltpu.SemaphoreType.DMA((copies,))] * (copies > 0),
        compiler_params=PARAMS,
    )(*scalars, *held, *fetched)


def room(*arrays):
    return [pltpu.VMEM(a.shape, a.dtype) for a in arrays]


def body(
    cells, cotangent, cell_count, first_norm_gain, first_norm_bias, w_fx, w_x, w_slice, temper,
    query_weight, key_weight, value_weight, w_out, second_norm_gain, second_norm_bias, w_up, w_down,
):
    rows, cot = cells[0], cotangent[0]
    core = lax.axis_index("c").astype(jnp.int32).reshape(1)
    gain1, bias1 = first_norm_gain.reshape(1, WIDTH), first_norm_bias.reshape(1, WIDTH)
    gain2, bias2 = second_norm_gain.reshape(1, WIDTH), second_norm_bias.reshape(1, WIDTH)
    tall, tall_b = ((WIDTH, CELLS), F32), ((WIDTH, CELLS), BF16)
    square = ((WIDTH, WIDTH), F32)
    pay, feats, mids, weights, stats = call(
        front_kernel, "front",
        [((40, 512), F32), tall_b, tall_b, ((512, CELLS), BF16), ((16, CELLS), F32)],
        [cell_count], [], [temper, rows, gain1, bias1, w_fx, w_x, w_slice, gain2, bias2],
        [pltpu.SMEM((HEADS,), F32)]
        + room(rows, gain1, bias1, w_fx, w_x, w_slice, gain2, bias2), copies=9,
    )
    pay = space_sum(pay)
    tok, gres, gs, keep2, send2, ln2, mix, xt, layer = call(
        middle_kernel, "middle",
        [((HEAD, 512), F32), tall, tall_b, ((LATE_HALF, 128), F32), ((LATE_HALF, 128), F32),
         ((8, WIDTH), F32), ((296, 512), F32), tall_b, ((CELLS, WIDTH), BF16)],
        [core],
        [pay, query_weight, key_weight, value_weight, weights, stats, rows, cot, w_out, w_up, w_down],
        (), room(rows), left=1, copies=1,
    )
    tok = space_sum(tok)
    late = keep2 + swap(send2, OTHER_CORE)
    keep3, send3, out_rows = call(
        rear_kernel, "rear",
        [((EARLY_HALF, 128), F32), ((EARLY_HALF, 128), F32), ((CELLS, WIDTH), BF16)],
        [core, temper],
        [tok, mix, query_weight, key_weight, value_weight, feats, mids, gs, weights, xt, stats, gres,
         ln2, w_fx, w_x, w_slice],
    )
    early = keep3 + swap(send3, OTHER_CORE)
    both = jnp.concatenate(
        [late.reshape(16, LATE_PART, 128), early.reshape(16, EARLY_PART, 128)], axis=1
    )
    part = jnp.sum(lax.all_to_all(both, PLANE, 0, 0), axis=0)
    for pairs in (Z_ONE, Z_TWO, Z_FAR):
        part = part + swap(part, pairs)
    mine = lax.all_to_all(jnp.broadcast_to(part[None], both.shape), PLANE, 0, 0)
    theirs = swap(mine, OTHER_CORE)
    fx, gx, out, up, down, sl, q, k, v, temp, dg1, db1, dg2, db2 = call(
        last_kernel, "last",
        [square] * 5 + [((HEAD, SLICES), F32)] + [((HEAD, HEAD), F32)] * 3 + [((1, HEADS), F32)]
        + [((1, WIDTH), F32)] * 4,
        [core], [mine, theirs], (),
        [pltpu.VMEM((LATE_HALF + EARLY_HALF, WIDTH), F32)],
    )
    flat = lambda a: a.reshape(WIDTH)
    return (
        layer[None], out_rows[None], flat(dg1), flat(db1), fx, gx, sl, temp.reshape(HEADS), q, k, v, out,
        flat(dg2), flat(db2), up, down,
    )


def solution(mesh):
    fine = Mesh(mesh.devices.reshape(2, 4, 2, 8, 2), AXES)
    split = P(("yl", "x"), ("yh", "z", "c"), None)
    return jax.shard_map(
        body,
        mesh=fine,
        in_specs=(split, split, P(("yl", "x"), ("yh", "z", "c"))) + (P(),) * 14,
        out_specs=(split, split) + (P(),) * 14,
        check_vma=False,
    )
```

```python
import math

import jax
import jax.numpy as jnp
from jax import lax
from jax.experimental import pallas as pl
from jax.experimental.pallas import tpu as pltpu
from jax.sharding import Mesh, PartitionSpec as P

WIDTH = 256
HEADS = 8
SLICES = 64
HEAD = 32
CELLS = 1024
PAIRS = HEADS // 2
EPS = 1e-05
F32 = jnp.float32
BF16 = jnp.bfloat16
AXES = ("yl", "x", "yh", "z", "c")
PLANE = ("yl", "x", "yh")
SPACE = 32
Z_SCALE = 1.0 / math.sqrt(8 * 32768)
LATE, EARLY = 1536, 1280
LATE_HALF, EARLY_HALF = LATE // 2, EARLY // 2
LATE_PART, EARLY_PART = LATE_HALF // 16, EARLY_HALF // 16


def nn(a, b, precision=None):
    return lax.dot_general(
        a, b, (((1,), (0,)), ((), ())), precision=precision, preferred_element_type=F32
    )


def nt(a, b, precision=None):
    return lax.dot_general(
        a, b, (((1,), (1,)), ((), ())), precision=precision, preferred_element_type=F32
    )


def exact(f, a, b):
    return f(a, b, precision=lax.Precision.HIGH)


def turned(w):
    return w.astype(F32).T.astype(BF16)


def lane_half(rows):
    return lax.broadcasted_iota(jnp.int32, (rows, 128), 1) < SLICES


def diagonal_128():
    row = lax.broadcasted_iota(jnp.int32, (128, 128), 0) < SLICES
    lane = lax.broadcasted_iota(jnp.int32, (128, 128), 1) < SLICES
    return row == lane


def spread_pair(t):
    first = lane_half(HEAD)
    return jnp.concatenate([jnp.where(first, t, 0.0), jnp.where(first, 0.0, t)], axis=0)


def fold_pair(d):
    return jnp.where(lane_half(HEAD), d[:HEAD], d[HEAD:])


def slice_pair(w_slice):
    w = w_slice.astype(F32)
    return spread_pair(jnp.concatenate([w, w], axis=1))


def norm_stats(xt):
    mean = jnp.sum(xt, axis=0, keepdims=True) * (1.0 / WIDTH)
    centred = xt - mean
    inv = lax.rsqrt(jnp.sum(centred * centred, axis=0, keepdims=True) * (1.0 / WIDTH) + EPS)
    return mean, inv, centred * inv


def norm_back(g, xhat, inv, gain):
    ng = g * gain
    m1 = jnp.sum(ng, axis=0, keepdims=True) * (1.0 / WIDTH)
    m2 = jnp.sum(ng * xhat, axis=0, keepdims=True) * (1.0 / WIDTH)
    return inv * (ng - m1 - xhat * m2)


def lanes128(v):
    return sum(v[:, i : i + 128] for i in range(128, CELLS, 128)) + v[:, :128]


def live_row(count):
    return (lax.broadcasted_iota(jnp.int32, (1, CELLS), 1) < count).astype(F32)


def as_row(column128):
    return jnp.sum(column128.T, axis=0, keepdims=True)


def as_column(row):
    return jnp.broadcast_to(row, (128, row.shape[1])).T[:, 0:1]


def inverse_temper(temper_ref):
    return [1.0 / jnp.full((1, CELLS), temper_ref[h], F32) for h in range(HEADS)]


def fetch(sources, targets, sems):
    copies = [
        pltpu.make_async_copy(source, target, sems.at[i])
        for i, (source, target) in enumerate(zip(sources, targets))
    ]
    for copy in copies:
        copy.start()
    return copies


def front_kernel(
    count_ref, temper_hbm, cells_hbm, gain_hbm, bias_hbm, wfx_hbm, wx_hbm, wsl_hbm, gain2_hbm,
    bias2_hbm, wq_hbm, wk_hbm, wv_hbm,
    pay_ref, feats_ref, mids_ref, weights_ref, stats_ref,
    temper_ref, cells_ref, gain_ref, bias_ref, wfx_ref, wx_ref, wsl_ref, gain2_ref, bias2_ref,
    wq_ref, wk_ref, wv_ref, sems,
):
    copies = fetch(
        (cells_hbm, wx_hbm, wsl_hbm, gain_hbm, bias_hbm, wfx_hbm, temper_hbm, gain2_hbm, bias2_hbm,
         wq_hbm, wk_hbm, wv_hbm),
        (cells_ref, wx_ref, wsl_ref, gain_ref, bias_ref, wfx_ref, temper_ref, gain2_ref, bias2_ref,
         wq_ref, wk_ref, wv_ref),
        sems,
    )
    ones = jnp.ones((16, CELLS), BF16)
    for copy in copies:
        copy.wait()
    pair = slice_pair(wsl_ref[...])
    for i in range(8):
        stats_ref[24:32, 128 * i : 128 * i + 128] = pair[8 * i : 8 * i + 8]
    pair_t = pair.T.astype(BF16)
    inv_t = inverse_temper(temper_ref)
    for h in range(HEADS):
        stats_ref[16 + h : 17 + h, :] = inv_t[h]
    xt = cells_ref[...].astype(F32).T
    mean, inv, xhat = norm_stats(xt)
    n1 = (xhat * as_column(gain_ref[...]) + as_column(bias_ref[...])).astype(BF16)
    mids = nn(turned(wx_ref[...]), n1).astype(BF16)
    feats = nn(turned(wfx_ref[...]), n1).astype(BF16)
    mids_ref[...] = mids
    feats_ref[...] = feats
    live = live_row(count_ref[0, 0])
    stats_ref[14:15, :] = live
    stats_ref[0:1, :] = mean
    stats_ref[1:2, :] = inv
    for i, ref in enumerate((gain_ref, bias_ref, gain2_ref, bias2_ref)):
        stats_ref[10 + i : 11 + i, 0:WIDTH] = ref[...]
    stats_ref[32:64, 0:128] = jnp.concatenate(
        [wq_ref[...], wk_ref[...], wv_ref[...], jnp.zeros((HEAD, HEAD), F32)], axis=1
    )
    for p in range(PAIRS):
        rows = slice(64 * p, 64 * p + 64)
        logits = nn(pair_t, mids[rows])
        halves = []
        for k in range(2):
            h = 2 * p + k
            l = logits[64 * k : 64 * k + 64] * inv_t[h]
            m = jnp.max(l, axis=0, keepdims=True)
            e = jnp.exp(l - m)
            s = jnp.sum(e, axis=0, keepdims=True)
            halves.append((e * (live / s)).astype(BF16))
            stats_ref[2 + h : 3 + h, :] = m + jnp.log(s)
        w = jnp.concatenate(halves, axis=0)
        weights_ref[128 * p : 128 * p + 128, :] = w
        d = nt(jnp.concatenate([feats[rows], ones], axis=0), w)
        pay_ref[32 * p : 32 * p + 32, :] = fold_pair(d[:64])
        pay_ref[128 + p : 129 + p, :] = d[64:65]
    pay_ref[132:136, :] = jnp.zeros((4, 128), F32)


def keep_kernel(wout_hbm, wup_hbm, wdown_hbm, cells_hbm, cot_hbm, near_ref, sems):
    sources = (wout_hbm, wup_hbm, wdown_hbm, cells_hbm, cot_hbm)
    places = ((0, 256), (256, 256), (512, 256), (768, CELLS), (1792, CELLS))
    targets = [near_ref.at[pl.ds(start, size), :] for start, size in places]
    for copy in fetch(sources, targets, sems):
        copy.wait()


def middle_kernel(
    core_ref, mine_ref, theirs_ref, weights_ref, stats_ref, near_ref,
    tok_ref, gres_ref, gs_ref, keep_ref, send_ref, ln2_ref, mix_ref, xt_ref, layer_hbm,
    layer_ref, pay_ref, sems,
):
    wout_ref = near_ref.at[0:256, :]
    wup_ref = near_ref.at[256:512, :]
    wdown_ref = near_ref.at[512:768, :]
    cells_ref = near_ref.at[768:1792, :]
    cot_ref = near_ref.at[1792:2816, :]
    maps = stats_ref[32:64, 0:128]
    wq, wk, wv = maps[:, 0:32], maps[:, 32:64], maps[:, 64:96]
    pay_ref[...] = mine_ref[...] + theirs_ref[...]
    gt = cot_ref[...].astype(F32).T.astype(BF16)
    g_act = nn(wdown_ref[...], gt)
    core = core_ref[0]
    lifted = jnp.concatenate([pay_ref[128 + p : 129 + p, :] for p in range(PAIRS)], axis=1) + EPS
    tok = jnp.concatenate([pay_ref[32 * p : 32 * p + 32, :] for p in range(PAIRS)], axis=1) / lifted
    qt = exact(nn, wq.T, tok)
    kt = exact(nn, wk.T, tok)
    vt = exact(nn, wv.T, tok)
    mix_ref[0:32, :] = tok
    mix_ref[32:64, :] = qt
    mix_ref[64:96, :] = kt
    mix_ref[96:128, :] = vt
    mix_ref[288:296, :] = jnp.broadcast_to(lifted, (8, 512))
    diagonal = diagonal_128()

    def give(at, grad):
        left = grad[:, :128] * Z_SCALE
        right = grad[:, 128:] * Z_SCALE
        keep_ref[at : at + 256, :] = jnp.where(core == 0, left, right)
        send_ref[at : at + 256, :] = jnp.where(core == 0, right, left)

    spread = []
    for p in range(PAIRS):
        lanes = slice(128 * p, 128 * p + 128)
        scores = exact(nn, kt[:, lanes].T, qt[:, lanes]) * (HEAD**-0.5)
        scores = jnp.where(diagonal, scores, -1e30)
        e = jnp.exp(scores - jnp.max(scores, axis=0, keepdims=True))
        e = jnp.where(diagonal, e, 0.0)
        attn = e / jnp.sum(e, axis=0, keepdims=True)
        mixed = exact(nn, vt[:, lanes], attn)
        mix_ref[128:256, lanes] = attn
        mixed = mixed.astype(BF16).astype(F32)
        mix_ref[256:288, lanes] = mixed
        spread.append(
            nn(spread_pair(mixed).astype(BF16), weights_ref[128 * p : 128 * p + 128, :])
        )
    xt = cells_ref[...].astype(F32).T
    xt_ref[...] = xt.astype(BF16)
    gain = as_column(stats_ref[12:13, 0:WIDTH])
    bias = as_column(stats_ref[13:14, 0:WIDTH])
    c0 = math.sqrt(2.0 / math.pi)
    spread = jnp.concatenate(spread, axis=0).astype(BF16)
    resid = (xt + nn(turned(wout_ref[...]), spread)).astype(BF16)
    _, inv, xhat = norm_stats(resid.astype(F32))
    n2 = (xhat * gain + bias).astype(BF16)
    up = nn(turned(wup_ref[...]), n2)
    sq = up * up
    t = jnp.tanh(c0 * up * (1.0 + 0.044715 * sq))
    half = 0.5 * (1.0 + t)
    act = (up * half).astype(BF16)
    layer = resid.astype(F32) + nn(turned(wdown_ref[...]), act)
    layer_ref[...] = layer.T.astype(BF16)
    (leave,) = fetch((layer_ref,), (layer_hbm,), sems)
    give(512, nt(act, gt))
    slope = half + 0.5 * up * (1.0 - t * t) * (c0 * (1.0 + 3.0 * 0.044715 * sq))
    g_up = (slope * g_act).astype(BF16)
    give(256, nt(n2, g_up))
    g_n2 = nn(wup_ref[...], g_up)
    ln2_ref[0:1, :] = as_row(lanes128(g_n2 * xhat))
    ln2_ref[1:2, :] = as_row(lanes128(g_n2))
    gres = gt.astype(F32) + norm_back(g_n2, xhat, inv, gain)
    gres_ref[...] = gres
    gres_b = gres.astype(BF16)
    give(0, nt(spread, gres_b))
    gs = nn(wout_ref[...], gres_b).astype(BF16)
    gs_ref[...] = gs
    for p in range(PAIRS):
        d = nt(gs[64 * p : 64 * p + 64], weights_ref[128 * p : 128 * p + 128, :])
        tok_ref[:, 128 * p : 128 * p + 128] = fold_pair(d)
    leave.wait()


def rear_kernel(
    core_ref, mine_ref, theirs_ref, mix_ref, feats_ref, mids_ref,
    gs_ref, weights_ref, xt_ref, stats_ref, ln2_ref,
    wfx_ref, wx_ref,
    keep_ref, send_ref, g_n1_ref,
):
    core = core_ref[0]
    lifted = mix_ref[288:289, :]
    tok = mix_ref[0:32, :]
    qt = mix_ref[32:64, :]
    kt = mix_ref[64:96, :]
    vt = mix_ref[96:128, :]
    dqs, dks, dvs = [], [], []
    for p in range(PAIRS):
        lanes = slice(128 * p, 128 * p + 128)
        gm = mine_ref[:, lanes] + theirs_ref[:, lanes]
        attn = mix_ref[128:256, lanes]
        da = exact(nn, vt[:, lanes].T, gm)
        dvs.append(exact(nt, gm, attn))
        pulled = attn * da
        ds = (pulled - attn * jnp.sum(pulled, axis=0, keepdims=True)) * (HEAD**-0.5)
        dqs.append(exact(nn, kt[:, lanes], ds))
        dks.append(exact(nt, qt[:, lanes], ds))
    dq = jnp.concatenate(dqs, axis=1)
    dk = jnp.concatenate(dks, axis=1)
    dv = jnp.concatenate(dvs, axis=1)
    maps = stats_ref[32:64, 0:128]
    dtok = (
        exact(nn, maps[:, 0:32], dq) + exact(nn, maps[:, 32:64], dk) + exact(nn, maps[:, 64:96], dv)
    )
    qkv = exact(nt, tok, jnp.concatenate([dq, dk, dv, jnp.zeros_like(dq)], axis=0))
    gnum = (dtok / lifted).astype(BF16).astype(F32)
    gden = -jnp.sum(dtok * tok, axis=0, keepdims=True) / lifted

    live = stats_ref[14:15, :]
    pair = jnp.concatenate(
        [stats_ref[24:32, 128 * i : 128 * i + 128] for i in range(8)], axis=0
    )
    pair_b = pair.astype(BF16)
    pair_t = pair.T.astype(BF16)
    inv_t = [stats_ref[16 + h : 17 + h, :] for h in range(HEADS)]
    g_mids, g_feats, temps, slices = [], [], [], 0.0
    for p in range(PAIRS):
        lanes = slice(128 * p, 128 * p + 128)
        rows = slice(64 * p, 64 * p + 64)
        num = spread_pair(gnum[:, lanes])
        g_feats.append(nn(num.astype(BF16), weights_ref[lanes, :]))
        both = jnp.concatenate([spread_pair(mix_ref[256:288, lanes]), num], axis=0)
        gw = nn(
            both.T.astype(BF16), jnp.concatenate([gs_ref[rows, :], feats_ref[rows, :]], axis=0)
        )
        den = as_column(gden[:, lanes])
        logits = nn(pair_t, mids_ref[rows, :])
        scaled = []
        for k in range(2):
            h = 2 * p + k
            part = slice(64 * k, 64 * k + 64)
            l = logits[part] * inv_t[h]
            pr = jnp.exp(l - stats_ref[2 + h : 3 + h, :]) * live
            pulled = (gw[part] + den[part]) * pr
            gl = pulled - pr * jnp.sum(pulled, axis=0, keepdims=True)
            temps.append(jnp.sum(gl * l, axis=0, keepdims=True))
            scaled.append((gl * inv_t[h]).astype(BF16))
        scaled = jnp.concatenate(scaled, axis=0)
        g_mids.append(nn(pair_b, scaled))
        slices = slices + fold_pair(nt(mids_ref[rows, :], scaled))
    g_mids = jnp.concatenate(g_mids, axis=0).astype(BF16)
    g_feats = jnp.concatenate(g_feats, axis=0).astype(BF16)
    gain = as_column(stats_ref[10:11, 0:WIDTH])
    inv = stats_ref[1:2, :]
    xhat = (xt_ref[...].astype(F32) - stats_ref[0:1, :]) * inv
    n1 = (xhat * gain + as_column(stats_ref[11:12, 0:WIDTH])).astype(BF16)
    grad_fx = nt(n1, g_feats)
    grad_x = nt(n1, g_mids)
    g_n1 = nn(wfx_ref[...], g_feats) + nn(wx_ref[...], g_mids)
    g_n1_ref[...] = g_n1
    slices = slices + pltpu.roll(slices, 64, 1)
    inv_col = jnp.concatenate([t[:, :128] for t in inv_t], axis=0)
    temps = jnp.sum(lanes128(jnp.concatenate(temps, axis=0)), axis=1, keepdims=True)
    temper = -jnp.broadcast_to(temps, (8, 128)) * inv_col
    rows = jnp.concatenate(
        [as_row(lanes128(g_n1 * xhat)), as_row(lanes128(g_n1)), ln2_ref[0:2, :],
         jnp.zeros((4, WIDTH), F32)],
        axis=0,
    )

    def give(at, left, right):
        left = left * Z_SCALE
        right = right * Z_SCALE
        keep_ref[at : at + left.shape[0], :] = jnp.where(core == 0, left, right)
        send_ref[at : at + left.shape[0], :] = jnp.where(core == 0, right, left)

    give(0, grad_fx[:, :128], grad_fx[:, 128:])
    give(256, grad_x[:, :128], grad_x[:, 128:])
    give(512, slices, qkv * (1.0 / SPACE))
    give(544, temper, jnp.zeros((8, 128), F32))
    give(552, rows[:, :128], rows[:, 128:])
    nothing = jnp.zeros((EARLY_HALF - 560, 128), F32)
    give(560, nothing, nothing)


def cells_kernel(g_n1_ref, xt_ref, gres_ref, stats_ref, out_ref):
    inv = stats_ref[1:2, :]
    xhat = (xt_ref[...].astype(F32) - stats_ref[0:1, :]) * inv
    gain = as_column(stats_ref[10:11, 0:WIDTH])
    out_ref[...] = (gres_ref[...] + norm_back(g_n1_ref[...], xhat, inv, gain)).T.astype(BF16)


def last_kernel(
    core_ref, mine_ref, theirs_ref,
    fx_ref, x_ref, out_ref, up_ref, down_ref, slice_ref, q_ref, k_ref, v_ref, temper_ref, gain1_ref, bias1_ref,
    gain2_ref, bias2_ref,
    whole_ref,
):
    core = core_ref[0]
    for part in range(16):
        mine = mine_ref[part]
        theirs = theirs_ref[part]
        left = jnp.where(core == 0, mine, theirs)
        right = jnp.where(core == 0, theirs, mine)
        both = jnp.concatenate([left, right], axis=1)
        whole_ref[part * LATE_PART : (part + 1) * LATE_PART, :] = both[:LATE_PART]
        at = LATE_HALF + part * EARLY_PART
        whole_ref[at : at + EARLY_PART, :] = both[LATE_PART:]
    out_ref[...] = whole_ref[0:256, :]
    up_ref[...] = whole_ref[256:512, :]
    down_ref[...] = whole_ref[512:768, :]
    fx_ref[...] = whole_ref[768:1024, :]
    x_ref[...] = whole_ref[1024:1280, :]
    slice_ref[...] = whole_ref[1280:1312, 0:64]
    qkv = whole_ref[1280:1312, 128:256]
    q_ref[...] = qkv[:, 0:32]
    k_ref[...] = qkv[:, 32:64]
    v_ref[...] = qkv[:, 64:96]
    temper_ref[...] = whole_ref[1312:1320, 0:128].T[0:1, :]
    gain1_ref[...] = whole_ref[1320:1321, :]
    bias1_ref[...] = whole_ref[1321:1322, :]
    gain2_ref[...] = whole_ref[1322:1323, :]
    bias2_ref[...] = whole_ref[1323:1324, :]


def permutation(move):
    pairs = []
    for yl in range(2):
        for x in range(4):
            for yh in range(2):
                for z in range(8):
                    for c in range(2):
                        place = lambda a, b, e, f, g: (((a * 4 + b) * 2 + e) * 8 + f) * 2 + g
                        pairs.append((place(yl, x, yh, z, c), place(*move(yl, x, yh, z, c))))
    return pairs


OTHER_CORE = permutation(lambda yl, x, yh, z, c: (yl, x, yh, z, 1 - c))
Z_ONE = permutation(lambda yl, x, yh, z, c: (yl, x, yh, z ^ 1, c))
Z_TWO = permutation(lambda yl, x, yh, z, c: (yl, x, yh, z ^ 2, c))
Z_FAR = permutation(lambda yl, x, yh, z, c: (yl, x, yh, 7 - z, c))
Y_FAR = permutation(lambda yl, x, yh, z, c: (yl, x, 1 - yh, z, c))


def swap(v, pairs):
    return lax.ppermute(v, AXES, pairs)


def near_sum(v):
    for pairs in (OTHER_CORE, Z_ONE, Z_TWO, Z_FAR):
        v = v + swap(v, pairs)
    return v


VMEM = pl.BlockSpec(memory_space=pltpu.VMEM)
SMEM = pl.BlockSpec(memory_space=pltpu.SMEM)
HBM = pl.BlockSpec(memory_space=pltpu.HBM)
PARAMS = pltpu.CompilerParams(vmem_limit_bytes=16 * 1024 * 1024)


def call(kernel, name, outs, scalars, held, fetched=(), scratch=(), left=0, copies=0):
    near = len(outs) - left
    fetched = [pltpu.with_memory_space_constraint(a, pltpu.HBM) for a in fetched]
    return pl.pallas_call(
        kernel,
        name=name,
        out_shape=[jax.ShapeDtypeStruct(shape, dtype) for shape, dtype in outs],
        in_specs=[SMEM] * len(scalars) + [VMEM] * len(held) + [HBM] * len(fetched),
        out_specs=[VMEM] * near + [HBM] * left,
        scratch_shapes=list(scratch) + [pltpu.SemaphoreType.DMA((copies,))] * (copies > 0),
        compiler_params=PARAMS,
    )(*scalars, *held, *fetched)


def room(*arrays):
    return [pltpu.VMEM(a.shape, a.dtype) for a in arrays]


def body(
    cells, cotangent, cell_count, first_norm_gain, first_norm_bias, w_fx, w_x, w_slice, temper,
    query_weight, key_weight, value_weight, w_out, second_norm_gain, second_norm_bias, w_up, w_down,
):
    rows, cot = cells[0], cotangent[0]
    core = lax.axis_index("c").astype(jnp.int32).reshape(1)
    gain1, bias1 = first_norm_gain.reshape(1, WIDTH), first_norm_bias.reshape(1, WIDTH)
    gain2, bias2 = second_norm_gain.reshape(1, WIDTH), second_norm_bias.reshape(1, WIDTH)
    tall, tall_b = ((WIDTH, CELLS), F32), ((WIDTH, CELLS), BF16)
    square = ((WIDTH, WIDTH), F32)
    pay, feats, mids, weights, stats = call(
        front_kernel, "front",
        [((136, 128), F32), tall_b, tall_b, ((512, CELLS), BF16), ((64, CELLS), F32)],
        [cell_count], [], [temper, rows, gain1, bias1, w_fx, w_x, w_slice, gain2, bias2,
         query_weight, key_weight, value_weight],
        [pltpu.SMEM((HEADS,), F32)]
        + room(rows, gain1, bias1, w_fx, w_x, w_slice, gain2, bias2, query_weight, key_weight,
               value_weight),
        copies=12,
    )
    for pairs in (OTHER_CORE, Z_ONE):
        pay = pay + swap(pay, pairs)
    (near,) = call(
        keep_kernel, "keep", [((2816, WIDTH), BF16)], [], [], [w_out, w_up, w_down, rows, cot], copies=5
    )
    got, near = lax.optimization_barrier((swap(pay, Z_TWO), near))
    pay = pay + got
    pay = pay + swap(pay, Z_FAR)
    tok, gres, gs, keep2, send2, ln2, mix, xt, layer = call(
        middle_kernel, "middle",
        [((HEAD, 512), F32), tall, tall_b, ((LATE_HALF, 128), F32), ((LATE_HALF, 128), F32),
         ((8, WIDTH), F32), ((296, 512), F32), tall_b, ((CELLS, WIDTH), BF16)],
        [core],
        [pay, swap(pay, Y_FAR), weights, stats, near],
        (), room(rows) + [pltpu.VMEM((136, 128), F32)], left=1, copies=1,
    )
    tok = near_sum(tok)
    late = keep2 + swap(send2, OTHER_CORE)
    keep3, send3, g_n1 = call(
        rear_kernel, "rear",
        [((EARLY_HALF, 128), F32), ((EARLY_HALF, 128), F32), tall],
        [core],
        [tok, swap(tok, Y_FAR), mix, feats, mids, gs, weights,
         xt, stats, ln2, w_fx, w_x],
    )
    (out_rows,) = call(
        cells_kernel, "cells", [((CELLS, WIDTH), BF16)], [], [g_n1, xt, gres, stats]
    )
    swapped, out_rows = lax.optimization_barrier((swap(send3, OTHER_CORE), out_rows))
    early = keep3 + swapped
    both = jnp.concatenate(
        [late.reshape(16, LATE_PART, 128), early.reshape(16, EARLY_PART, 128)], axis=1
    )
    part = jnp.sum(lax.all_to_all(both, PLANE, 0, 0), axis=0)
    for pairs in (Z_ONE, Z_TWO, Z_FAR):
        part = part + swap(part, pairs)
    mine = lax.all_to_all(jnp.broadcast_to(part[None], both.shape), PLANE, 0, 0)
    theirs = swap(mine, OTHER_CORE)
    fx, gx, out, up, down, sl, q, k, v, temp, dg1, db1, dg2, db2 = call(
        last_kernel, "last",
        [square] * 5 + [((HEAD, SLICES), F32)] + [((HEAD, HEAD), F32)] * 3 + [((1, HEADS), F32)]
        + [((1, WIDTH), F32)] * 4,
        [core], [mine, theirs], (),
        [pltpu.VMEM((LATE_HALF + EARLY_HALF, WIDTH), F32)],
    )
    flat = lambda a: a.reshape(WIDTH)
    return (
        layer[None], out_rows[None], flat(dg1), flat(db1), fx, gx, sl, temp.reshape(HEADS), q, k, v, out,
        flat(dg2), flat(db2), up, down,
    )


def solution(mesh):
    fine = Mesh(mesh.devices.reshape(2, 4, 2, 8, 2), AXES)
    split = P(("yl", "x"), ("yh", "z", "c"), None)
    return jax.shard_map(
        body,
        mesh=fine,
        in_specs=(split, split, P(("yl", "x"), ("yh", "z", "c"))) + (P(),) * 14,
        out_specs=(split, split) + (P(),) * 14,
        check_vma=False,
    )
```

```python
import math

import jax
import jax.numpy as jnp
from jax import lax
from jax.experimental import pallas as pl
from jax.experimental.pallas import tpu as pltpu
from jax.sharding import Mesh, PartitionSpec as P

WIDTH = 256
HEADS = 8
SLICES = 64
HEAD = 32
CELLS = 1024
PAIRS = HEADS // 2
EPS = 1e-05
F32 = jnp.float32
BF16 = jnp.bfloat16
AXES = ("yl", "x", "yh", "z", "c")
PLANE = ("yl", "x", "yh")
SPACE = 32
Z_SCALE = 1.0 / math.sqrt(8 * 32768)
LATE, EARLY = 1536, 1280
LATE_HALF, EARLY_HALF = LATE // 2, EARLY // 2
LATE_PART, EARLY_PART = LATE_HALF // 16, EARLY_HALF // 16


def nn(a, b, precision=None):
    return lax.dot_general(
        a, b, (((1,), (0,)), ((), ())), precision=precision, preferred_element_type=F32
    )


def nt(a, b, precision=None):
    return lax.dot_general(
        a, b, (((1,), (1,)), ((), ())), precision=precision, preferred_element_type=F32
    )


def exact(f, a, b):
    return f(a, b, precision=lax.Precision.HIGH)


def turned(w):
    return w.astype(F32).T.astype(BF16)


def lane_half(rows):
    return lax.broadcasted_iota(jnp.int32, (rows, 128), 1) < SLICES


def diagonal_128():
    row = lax.broadcasted_iota(jnp.int32, (128, 128), 0) < SLICES
    lane = lax.broadcasted_iota(jnp.int32, (128, 128), 1) < SLICES
    return row == lane


def spread_pair(t):
    first = lane_half(HEAD)
    return jnp.concatenate([jnp.where(first, t, 0.0), jnp.where(first, 0.0, t)], axis=0)


def fold_pair(d):
    return jnp.where(lane_half(HEAD), d[:HEAD], d[HEAD:])


def slice_pair(w_slice):
    w = w_slice.astype(F32)
    return spread_pair(jnp.concatenate([w, w], axis=1))


def norm_stats(xt):
    mean = jnp.sum(xt, axis=0, keepdims=True) * (1.0 / WIDTH)
    centred = xt - mean
    inv = lax.rsqrt(jnp.sum(centred * centred, axis=0, keepdims=True) * (1.0 / WIDTH) + EPS)
    return mean, inv, centred * inv


def norm_back(g, xhat, inv, gain):
    ng = g * gain
    m1 = jnp.sum(ng, axis=0, keepdims=True) * (1.0 / WIDTH)
    m2 = jnp.sum(ng * xhat, axis=0, keepdims=True) * (1.0 / WIDTH)
    return inv * (ng - m1 - xhat * m2)


def lanes128(v):
    return sum(v[:, i : i + 128] for i in range(128, CELLS, 128)) + v[:, :128]


def live_row(count):
    return (lax.broadcasted_iota(jnp.int32, (1, CELLS), 1) < count).astype(F32)


def as_row(column128):
    return jnp.sum(column128.T, axis=0, keepdims=True)


def as_column(row):
    return jnp.broadcast_to(row, (128, row.shape[1])).T[:, 0:1]


def inverse_temper(temper_ref):
    return [1.0 / jnp.full((1, CELLS), temper_ref[h], F32) for h in range(HEADS)]


def fetch(sources, targets, sems):
    copies = [
        pltpu.make_async_copy(source, target, sems.at[i])
        for i, (source, target) in enumerate(zip(sources, targets))
    ]
    for copy in copies:
        copy.start()
    return copies


def front_kernel(
    count_ref, temper_hbm, cells_hbm, gain_hbm, bias_hbm, wfx_hbm, wx_hbm, wsl_hbm, gain2_hbm,
    bias2_hbm, wq_hbm, wk_hbm, wv_hbm,
    pay_ref, feats_ref, mids_ref, weights_ref, stats_ref,
    temper_ref, cells_ref, gain_ref, bias_ref, wfx_ref, wx_ref, wsl_ref, gain2_ref, bias2_ref,
    wq_ref, wk_ref, wv_ref, sems,
):
    copies = fetch(
        (cells_hbm, wx_hbm, wsl_hbm, gain_hbm, bias_hbm, wfx_hbm, temper_hbm, gain2_hbm, bias2_hbm,
         wq_hbm, wk_hbm, wv_hbm),
        (cells_ref, wx_ref, wsl_ref, gain_ref, bias_ref, wfx_ref, temper_ref, gain2_ref, bias2_ref,
         wq_ref, wk_ref, wv_ref),
        sems,
    )
    ones = jnp.ones((16, CELLS), BF16)
    for copy in copies:
        copy.wait()
    pair = slice_pair(wsl_ref[...])
    for i in range(8):
        stats_ref[24:32, 128 * i : 128 * i + 128] = pair[8 * i : 8 * i + 8]
    pair_t = pair.T.astype(BF16)
    inv_t = inverse_temper(temper_ref)
    for h in range(HEADS):
        stats_ref[16 + h : 17 + h, :] = inv_t[h]
    xt = cells_ref[...].astype(F32).T
    mean, inv, xhat = norm_stats(xt)
    n1 = (xhat * as_column(gain_ref[...]) + as_column(bias_ref[...])).astype(BF16)
    mids = nn(turned(wx_ref[...]), n1).astype(BF16)
    feats = nn(turned(wfx_ref[...]), n1).astype(BF16)
    mids_ref[...] = mids
    feats_ref[...] = feats
    live = live_row(count_ref[0, 0])
    stats_ref[14:15, :] = live
    stats_ref[0:1, :] = mean
    stats_ref[1:2, :] = inv
    for i, ref in enumerate((gain_ref, bias_ref, gain2_ref, bias2_ref)):
        stats_ref[10 + i : 11 + i, 0:WIDTH] = ref[...]
    stats_ref[32:64, 0:128] = jnp.concatenate(
        [wq_ref[...], wk_ref[...], wv_ref[...], jnp.zeros((HEAD, HEAD), F32)], axis=1
    )
    for p in range(PAIRS):
        rows = slice(64 * p, 64 * p + 64)
        logits = nn(pair_t, mids[rows])
        halves = []
        for k in range(2):
            h = 2 * p + k
            l = logits[64 * k : 64 * k + 64] * inv_t[h]
            m = jnp.max(l, axis=0, keepdims=True)
            e = jnp.exp(l - m)
            s = jnp.sum(e, axis=0, keepdims=True)
            halves.append((e * (live / s)).astype(BF16))
            stats_ref[2 + h : 3 + h, :] = m + jnp.log(s)
        w = jnp.concatenate(halves, axis=0)
        weights_ref[128 * p : 128 * p + 128, :] = w
        d = nt(jnp.concatenate([feats[rows], ones], axis=0), w)
        pay_ref[32 * p : 32 * p + 32, :] = fold_pair(d[:64])
        pay_ref[128 + p : 129 + p, :] = d[64:65]
    pay_ref[132:136, :] = jnp.zeros((4, 128), F32)


def keep_kernel(wout_hbm, wup_hbm, wdown_hbm, cells_hbm, cot_hbm, near_ref, sems):
    sources = (wout_hbm, wup_hbm, wdown_hbm, cells_hbm, cot_hbm)
    places = ((0, 256), (256, 256), (512, 256), (768, CELLS), (1792, CELLS))
    targets = [near_ref.at[pl.ds(start, size), :] for start, size in places]
    for copy in fetch(sources, targets, sems):
        copy.wait()


def middle_kernel(
    core_ref, mine_ref, theirs_ref, weights_ref, stats_ref, near_ref,
    tok_ref, gres_ref, gs_ref, keep_ref, send_ref, ln2_ref, mix_ref, xt_ref, layer_hbm,
    layer_ref, pay_ref, sems,
):
    wout_ref = near_ref.at[0:256, :]
    wup_ref = near_ref.at[256:512, :]
    wdown_ref = near_ref.at[512:768, :]
    cells_ref = near_ref.at[768:1792, :]
    cot_ref = near_ref.at[1792:2816, :]
    maps = stats_ref[32:64, 0:128]
    wq, wk, wv = maps[:, 0:32], maps[:, 32:64], maps[:, 64:96]
    pay_ref[...] = mine_ref[...] + theirs_ref[...]
    gt = cot_ref[...].astype(F32).T.astype(BF16)
    g_act = nn(wdown_ref[...], gt)
    core = core_ref[0]
    lifted = jnp.concatenate([pay_ref[128 + p : 129 + p, :] for p in range(PAIRS)], axis=1) + EPS
    tok = jnp.concatenate([pay_ref[32 * p : 32 * p + 32, :] for p in range(PAIRS)], axis=1) / lifted
    qt = exact(nn, wq.T, tok)
    kt = exact(nn, wk.T, tok)
    vt = exact(nn, wv.T, tok)
    mix_ref[0:32, :] = tok
    mix_ref[32:64, :] = qt
    mix_ref[64:96, :] = kt
    mix_ref[96:128, :] = vt
    mix_ref[288:296, :] = jnp.broadcast_to(lifted, (8, 512))
    diagonal = diagonal_128()

    def give(at, grad):
        left = grad[:, :128] * Z_SCALE
        right = grad[:, 128:] * Z_SCALE
        keep_ref[at : at + 256, :] = jnp.where(core == 0, left, right)
        send_ref[at : at + 256, :] = jnp.where(core == 0, right, left)

    spread = []
    for p in range(PAIRS):
        lanes = slice(128 * p, 128 * p + 128)
        scores = exact(nn, kt[:, lanes].T, qt[:, lanes]) * (HEAD**-0.5)
        scores = jnp.where(diagonal, scores, -1e30)
        e = jnp.exp(scores - jnp.max(scores, axis=0, keepdims=True))
        e = jnp.where(diagonal, e, 0.0)
        attn = e / jnp.sum(e, axis=0, keepdims=True)
        mixed = exact(nn, vt[:, lanes], attn)
        mix_ref[128:256, lanes] = attn
        mixed = mixed.astype(BF16).astype(F32)
        mix_ref[256:288, lanes] = mixed
        spread.append(
            nn(spread_pair(mixed).astype(BF16), weights_ref[128 * p : 128 * p + 128, :])
        )
    xt = cells_ref[...].astype(F32).T
    xt_ref[...] = xt.astype(BF16)
    gain = as_column(stats_ref[12:13, 0:WIDTH])
    bias = as_column(stats_ref[13:14, 0:WIDTH])
    c0 = math.sqrt(2.0 / math.pi)
    spread = jnp.concatenate(spread, axis=0).astype(BF16)
    resid = (xt + nn(turned(wout_ref[...]), spread)).astype(BF16)
    _, inv, xhat = norm_stats(resid.astype(F32))
    n2 = (xhat * gain + bias).astype(BF16)
    up = nn(turned(wup_ref[...]), n2)
    sq = up * up
    t = jnp.tanh(c0 * up * (1.0 + 0.044715 * sq))
    half = 0.5 * (1.0 + t)
    act = (up * half).astype(BF16)
    layer = resid.astype(F32) + nn(turned(wdown_ref[...]), act)
    layer_ref[...] = layer.T.astype(BF16)
    (leave,) = fetch((layer_ref,), (layer_hbm,), sems)
    give(512, nt(act, gt))
    slope = half + 0.5 * up * (1.0 - t * t) * (c0 * (1.0 + 3.0 * 0.044715 * sq))
    g_up = (slope * g_act).astype(BF16)
    give(256, nt(n2, g_up))
    g_n2 = nn(wup_ref[...], g_up)
    ln2_ref[0:1, :] = as_row(lanes128(g_n2 * xhat))
    ln2_ref[1:2, :] = as_row(lanes128(g_n2))
    gres = gt.astype(F32) + norm_back(g_n2, xhat, inv, gain)
    gres_ref[...] = gres
    gres_b = gres.astype(BF16)
    give(0, nt(spread, gres_b))
    gs = nn(wout_ref[...], gres_b).astype(BF16)
    gs_ref[...] = gs
    for p in range(PAIRS):
        d = nt(gs[64 * p : 64 * p + 64], weights_ref[128 * p : 128 * p + 128, :])
        tok_ref[:, 128 * p : 128 * p + 128] = fold_pair(d)
    leave.wait()


def rear_kernel(
    core_ref, mine_ref, theirs_ref, mix_ref, feats_ref, mids_ref,
    gs_ref, weights_ref, xt_ref, stats_ref, ln2_ref,
    wfx_ref, wx_ref,
    keep_ref, send_ref, g_n1_ref,
):
    core = core_ref[0]
    lifted = mix_ref[288:289, :]
    tok = mix_ref[0:32, :]
    qt = mix_ref[32:64, :]
    kt = mix_ref[64:96, :]
    vt = mix_ref[96:128, :]
    dqs, dks, dvs = [], [], []
    for p in range(PAIRS):
        lanes = slice(128 * p, 128 * p + 128)
        gm = mine_ref[:, lanes] + theirs_ref[:, lanes]
        attn = mix_ref[128:256, lanes]
        da = exact(nn, vt[:, lanes].T, gm)
        dvs.append(exact(nt, gm, attn))
        pulled = attn * da
        ds = (pulled - attn * jnp.sum(pulled, axis=0, keepdims=True)) * (HEAD**-0.5)
        dqs.append(exact(nn, kt[:, lanes], ds))
        dks.append(exact(nt, qt[:, lanes], ds))
    dq = jnp.concatenate(dqs, axis=1)
    dk = jnp.concatenate(dks, axis=1)
    dv = jnp.concatenate(dvs, axis=1)
    maps = stats_ref[32:64, 0:128]
    dtok = (
        exact(nn, maps[:, 0:32], dq) + exact(nn, maps[:, 32:64], dk) + exact(nn, maps[:, 64:96], dv)
    )
    qkv = exact(nt, tok, jnp.concatenate([dq, dk, dv, jnp.zeros_like(dq)], axis=0))
    gnum = (dtok / lifted).astype(BF16).astype(F32)
    gden = -jnp.sum(dtok * tok, axis=0, keepdims=True) / lifted

    live = stats_ref[14:15, :]
    pair = jnp.concatenate(
        [stats_ref[24:32, 128 * i : 128 * i + 128] for i in range(8)], axis=0
    )
    pair_b = pair.astype(BF16)
    pair_t = pair.T.astype(BF16)
    inv_t = [stats_ref[16 + h : 17 + h, :] for h in range(HEADS)]
    g_mids, g_feats, temps, slices = [], [], [], 0.0
    for p in range(PAIRS):
        lanes = slice(128 * p, 128 * p + 128)
        rows = slice(64 * p, 64 * p + 64)
        num = spread_pair(gnum[:, lanes])
        g_feats.append(nn(num.astype(BF16), weights_ref[lanes, :]))
        both = jnp.concatenate([spread_pair(mix_ref[256:288, lanes]), num], axis=0)
        gw = nn(
            both.T.astype(BF16), jnp.concatenate([gs_ref[rows, :], feats_ref[rows, :]], axis=0)
        )
        den = as_column(gden[:, lanes])
        logits = nn(pair_t, mids_ref[rows, :])
        scaled = []
        for k in range(2):
            h = 2 * p + k
            part = slice(64 * k, 64 * k + 64)
            l = logits[part] * inv_t[h]
            pr = jnp.exp(l - stats_ref[2 + h : 3 + h, :]) * live
            pulled = (gw[part] + den[part]) * pr
            gl = pulled - pr * jnp.sum(pulled, axis=0, keepdims=True)
            temps.append(jnp.sum(gl * l, axis=0, keepdims=True))
            scaled.append((gl * inv_t[h]).astype(BF16))
        scaled = jnp.concatenate(scaled, axis=0)
        g_mids.append(nn(pair_b, scaled))
        slices = slices + fold_pair(nt(mids_ref[rows, :], scaled))
    g_mids = jnp.concatenate(g_mids, axis=0).astype(BF16)
    g_feats = jnp.concatenate(g_feats, axis=0).astype(BF16)
    gain = as_column(stats_ref[10:11, 0:WIDTH])
    inv = stats_ref[1:2, :]
    xhat = (xt_ref[...].astype(F32) - stats_ref[0:1, :]) * inv
    n1 = (xhat * gain + as_column(stats_ref[11:12, 0:WIDTH])).astype(BF16)
    grad_fx = nt(n1, g_feats)
    grad_x = nt(n1, g_mids)
    g_n1 = nn(wfx_ref[...], g_feats) + nn(wx_ref[...], g_mids)
    g_n1_ref[...] = g_n1
    slices = slices + pltpu.roll(slices, 64, 1)
    inv_col = jnp.concatenate([t[:, :128] for t in inv_t], axis=0)
    temps = jnp.sum(lanes128(jnp.concatenate(temps, axis=0)), axis=1, keepdims=True)
    temper = -jnp.broadcast_to(temps, (8, 128)) * inv_col
    rows = jnp.concatenate(
        [as_row(lanes128(g_n1 * xhat)), as_row(lanes128(g_n1)), ln2_ref[0:2, :],
         jnp.zeros((4, WIDTH), F32)],
        axis=0,
    )

    def give(at, left, right):
        left = left * Z_SCALE
        right = right * Z_SCALE
        keep_ref[at : at + left.shape[0], :] = jnp.where(core == 0, left, right)
        send_ref[at : at + left.shape[0], :] = jnp.where(core == 0, right, left)

    give(0, grad_fx[:, :128], grad_fx[:, 128:])
    give(256, grad_x[:, :128], grad_x[:, 128:])
    give(512, slices, qkv * (1.0 / SPACE))
    give(544, temper, jnp.zeros((8, 128), F32))
    give(552, rows[:, :128], rows[:, 128:])
    nothing = jnp.zeros((EARLY_HALF - 560, 128), F32)
    give(560, nothing, nothing)


def cells_kernel(g_n1_ref, xt_ref, gres_ref, stats_ref, out_ref):
    inv = stats_ref[1:2, :]
    xhat = (xt_ref[...].astype(F32) - stats_ref[0:1, :]) * inv
    gain = as_column(stats_ref[10:11, 0:WIDTH])
    out_ref[...] = (gres_ref[...] + norm_back(g_n1_ref[...], xhat, inv, gain)).T.astype(BF16)


def last_kernel(
    core_ref, mine_ref, theirs_ref,
    fx_ref, x_ref, out_ref, up_ref, down_ref, slice_ref, q_ref, k_ref, v_ref, temper_ref, gain1_ref, bias1_ref,
    gain2_ref, bias2_ref,
    whole_ref,
):
    core = core_ref[0]
    for part in range(16):
        mine = mine_ref[part]
        theirs = theirs_ref[part]
        left = jnp.where(core == 0, mine, theirs)
        right = jnp.where(core == 0, theirs, mine)
        both = jnp.concatenate([left, right], axis=1)
        whole_ref[part * LATE_PART : (part + 1) * LATE_PART, :] = both[:LATE_PART]
        at = LATE_HALF + part * EARLY_PART
        whole_ref[at : at + EARLY_PART, :] = both[LATE_PART:]
    out_ref[...] = whole_ref[0:256, :]
    up_ref[...] = whole_ref[256:512, :]
    down_ref[...] = whole_ref[512:768, :]
    fx_ref[...] = whole_ref[768:1024, :]
    x_ref[...] = whole_ref[1024:1280, :]
    slice_ref[...] = whole_ref[1280:1312, 0:64]
    qkv = whole_ref[1280:1312, 128:256]
    q_ref[...] = qkv[:, 0:32]
    k_ref[...] = qkv[:, 32:64]
    v_ref[...] = qkv[:, 64:96]
    temper_ref[...] = whole_ref[1312:1320, 0:128].T[0:1, :]
    gain1_ref[...] = whole_ref[1320:1321, :]
    bias1_ref[...] = whole_ref[1321:1322, :]
    gain2_ref[...] = whole_ref[1322:1323, :]
    bias2_ref[...] = whole_ref[1323:1324, :]


def permutation(move):
    pairs = []
    for yl in range(2):
        for x in range(4):
            for yh in range(2):
                for z in range(8):
                    for c in range(2):
                        place = lambda a, b, e, f, g: (((a * 4 + b) * 2 + e) * 8 + f) * 2 + g
                        pairs.append((place(yl, x, yh, z, c), place(*move(yl, x, yh, z, c))))
    return pairs


OTHER_CORE = permutation(lambda yl, x, yh, z, c: (yl, x, yh, z, 1 - c))
Z_ONE = permutation(lambda yl, x, yh, z, c: (yl, x, yh, z ^ 1, c))
Z_TWO = permutation(lambda yl, x, yh, z, c: (yl, x, yh, z ^ 2, c))
Z_FAR = permutation(lambda yl, x, yh, z, c: (yl, x, yh, 7 - z, c))
Y_FAR = permutation(lambda yl, x, yh, z, c: (yl, x, 1 - yh, z, c))

BOTH_FAR = permutation(lambda yl, x, yh, z, c: (yl, x, 1 - yh, z ^ 2, c))


def swap(v, pairs):
    return lax.ppermute(v, AXES, pairs)


def near_sum(v):
    for pairs in (OTHER_CORE, Z_ONE):
        v = v + swap(v, pairs)
    return (v + swap(v, Z_TWO)) + (swap(v, Y_FAR) + swap(v, BOTH_FAR))


VMEM = pl.BlockSpec(memory_space=pltpu.VMEM)
SMEM = pl.BlockSpec(memory_space=pltpu.SMEM)
HBM = pl.BlockSpec(memory_space=pltpu.HBM)
PARAMS = pltpu.CompilerParams(vmem_limit_bytes=16 * 1024 * 1024)


def call(kernel, name, outs, scalars, held, fetched=(), scratch=(), left=0, copies=0):
    near = len(outs) - left
    fetched = [pltpu.with_memory_space_constraint(a, pltpu.HBM) for a in fetched]
    return pl.pallas_call(
        kernel,
        name=name,
        out_shape=[jax.ShapeDtypeStruct(shape, dtype) for shape, dtype in outs],
        in_specs=[SMEM] * len(scalars) + [VMEM] * len(held) + [HBM] * len(fetched),
        out_specs=[VMEM] * near + [HBM] * left,
        scratch_shapes=list(scratch) + [pltpu.SemaphoreType.DMA((copies,))] * (copies > 0),
        compiler_params=PARAMS,
    )(*scalars, *held, *fetched)


def room(*arrays):
    return [pltpu.VMEM(a.shape, a.dtype) for a in arrays]


def body(
    cells, cotangent, cell_count, first_norm_gain, first_norm_bias, w_fx, w_x, w_slice, temper,
    query_weight, key_weight, value_weight, w_out, second_norm_gain, second_norm_bias, w_up, w_down,
):
    rows, cot = cells[0], cotangent[0]
    core = lax.axis_index("c").astype(jnp.int32).reshape(1)
    gain1, bias1 = first_norm_gain.reshape(1, WIDTH), first_norm_bias.reshape(1, WIDTH)
    gain2, bias2 = second_norm_gain.reshape(1, WIDTH), second_norm_bias.reshape(1, WIDTH)
    tall, tall_b = ((WIDTH, CELLS), F32), ((WIDTH, CELLS), BF16)
    square = ((WIDTH, WIDTH), F32)
    pay, feats, mids, weights, stats = call(
        front_kernel, "front",
        [((136, 128), F32), tall_b, tall_b, ((512, CELLS), BF16), ((64, CELLS), F32)],
        [cell_count], [], [temper, rows, gain1, bias1, w_fx, w_x, w_slice, gain2, bias2,
         query_weight, key_weight, value_weight],
        [pltpu.SMEM((HEADS,), F32)]
        + room(rows, gain1, bias1, w_fx, w_x, w_slice, gain2, bias2, query_weight, key_weight,
               value_weight),
        copies=12,
    )
    for pairs in (OTHER_CORE, Z_ONE):
        pay = pay + swap(pay, pairs)
    (near,) = call(
        keep_kernel, "keep", [((2816, WIDTH), BF16)], [], [], [w_out, w_up, w_down, rows, cot], copies=5
    )
    two, far, both_far, near = lax.optimization_barrier(
        (swap(pay, Z_TWO), swap(pay, Y_FAR), swap(pay, BOTH_FAR), near)
    )
    pay = (pay + two) + (far + both_far)
    tok, gres, gs, keep2, send2, ln2, mix, xt, layer = call(
        middle_kernel, "middle",
        [((HEAD, 512), F32), tall, tall_b, ((LATE_HALF, 128), F32), ((LATE_HALF, 128), F32),
         ((8, WIDTH), F32), ((296, 512), F32), tall_b, ((CELLS, WIDTH), BF16)],
        [core],
        [pay, swap(pay, Z_FAR), weights, stats, near],
        (), room(rows) + [pltpu.VMEM((136, 128), F32)], left=1, copies=1,
    )
    tok = near_sum(tok)
    late = keep2 + swap(send2, OTHER_CORE)
    keep3, send3, g_n1 = call(
        rear_kernel, "rear",
        [((EARLY_HALF, 128), F32), ((EARLY_HALF, 128), F32), tall],
        [core],
        [tok, swap(tok, Z_FAR), mix, feats, mids, gs, weights,
         xt, stats, ln2, w_fx, w_x],
    )
    (out_rows,) = call(
        cells_kernel, "cells", [((CELLS, WIDTH), BF16)], [], [g_n1, xt, gres, stats]
    )
    swapped, out_rows = lax.optimization_barrier((swap(send3, OTHER_CORE), out_rows))
    early = keep3 + swapped
    both = jnp.concatenate(
        [late.reshape(16, LATE_PART, 128), early.reshape(16, EARLY_PART, 128)], axis=1
    )
    part = jnp.sum(lax.all_to_all(both, PLANE, 0, 0), axis=0)
    for pairs in (Z_ONE, Z_TWO, Z_FAR):
        part = part + swap(part, pairs)
    mine = lax.all_to_all(jnp.broadcast_to(part[None], both.shape), PLANE, 0, 0)
    theirs = swap(mine, OTHER_CORE)
    fx, gx, out, up, down, sl, q, k, v, temp, dg1, db1, dg2, db2 = call(
        last_kernel, "last",
        [square] * 5 + [((HEAD, SLICES), F32)] + [((HEAD, HEAD), F32)] * 3 + [((1, HEADS), F32)]
        + [((1, WIDTH), F32)] * 4,
        [core], [mine, theirs], (),
        [pltpu.VMEM((LATE_HALF + EARLY_HALF, WIDTH), F32)],
    )
    flat = lambda a: a.reshape(WIDTH)
    return (
        layer[None], out_rows[None], flat(dg1), flat(db1), fx, gx, sl, temp.reshape(HEADS), q, k, v, out,
        flat(dg2), flat(db2), up, down,
    )


def solution(mesh):
    fine = Mesh(mesh.devices.reshape(2, 4, 2, 8, 2), AXES)
    split = P(("yl", "x"), ("yh", "z", "c"), None)
    return jax.shard_map(
        body,
        mesh=fine,
        in_specs=(split, split, P(("yl", "x"), ("yh", "z", "c"))) + (P(),) * 14,
        out_specs=(split, split) + (P(),) * 14,
        check_vma=False,
    )
```
